32 devices in a mesh: dom: 32 (over z, y, x, core).
Axes of the slice: x: 2, y: 2, z: 4, core: 2. Of those that a mesh axis runs over, the one named last changes fastest.
Arguments:
- elevation: float32 [8192, 128], P('dom'), may hold values from -6 to 6
- momentum: float32 [8192, 2, 128], P('dom'), may hold values from -6 to 6
- depth: float32 [8192, 128], P('dom'), may hold values from 0.3 to 1.5
- drag: float32 [8192, 128], P('dom'), may hold values from 0.05 to 0.6
- div_weight: float32 [5, 2, 128, 128], replicated, may hold values from -0.078125 to 0.078125
- grad_weight: float32 [5, 128, 256], replicated, may hold values from -0.125 to 0.125
- neighbours: int32 [8192, 4], P('dom'), may hold values from 0 to 8191, as said below
- wet: int32 [4, 8192], P(None, 'dom'), may hold values from 0 to 1, as said below
- boundary_cells: int32 [8192], P('dom'), may hold values from 0 to 32767, as said below
- boundary_source: int32 [8192], P('dom'), may hold values from 0 to 4095
- series: float32 [4, 4096], P(None, 'dom'), may hold values from -6 to 6
- moved_from: int32 [8192], P('dom'), may hold values from 0 to 8191, as said below
Outputs:
- level_out: float32 [8192, 128], P('dom')
- flow_out: float32 [8192, 2, 128], P('dom')
The draws below stay inside these ranges and needn't reach their ends.
Inputs may be any that keep to these rules, and one draw needn't show every extreme that they name: Slots are left, right, lower, upper; the relation is mutual (b is c's right iff c is b's left, likewise lower and upper). Left and right neighbours lie on the block's own device; a lower neighbour lies on the block's own device or on the device of index one lower, an upper one on its own device or on the device of index one higher (wrapping around). No block has neighbours on both adjacent devices. Exactly 128 blocks of a device have a neighbour on the lower adjacent device, and exactly 128 on the upper one. 1 marks a block that is wet in that step. `boundary_cells`: block times 128 plus element, within the device that holds the entry; distinct within a device. `moved_from`: A permutation. The blocks that move from one device to one device (itself included) number at most 16, and some pair reaches that in every draw.
All inputs are finite; a program needn't handle non-finite values.
Results may differ from the reference program's by a relative error of at most 0.0001.
Values sent between devices are 32-bit elements; how exact they have to be, the bound alone decides.
A program may use at most 64 MiB of HBM per device.

```python
import math
import jax
import jax.numpy as jnp
from jax import lax

E = 128
ROW_BLOCKS = 128
BLK_DEV = 256
STEPS = 4
BND_DEV = 256
NBLK = 8192
NPAR = 4096
NBND = 8192
N_DOM = 32


def draw_neighbours(key, part):
    base = jax.random.fold_in(key, 101)
    ndevices = NBLK // BLK_DEV
    keys = jax.random.split(base, ndevices)
    shuffled = jax.vmap(lambda single: jax.random.permutation(single, BLK_DEV))(keys).astype(jnp.int32)
    offsets = jnp.arange(ndevices, dtype=jnp.int32)[:, None] * BLK_DEV
    grid_ids = (shuffled + offsets).reshape(-1, ROW_BLOCKS)
    left = jnp.roll(grid_ids, 1, axis=1)
    right = jnp.roll(grid_ids, -1, axis=1)
    lower = jnp.roll(grid_ids, 1, axis=0)
    upper = jnp.roll(grid_ids, -1, axis=0)
    stacked = jnp.stack([left, right, lower, upper], axis=-1).reshape(-1, 4)
    return jnp.zeros((NBLK, 4), jnp.int32).at[grid_ids.reshape(-1)].set(stacked)


def draw_wet(key, part):
    base = jax.random.fold_in(key, 202)
    first, second = jax.random.split(base)
    ndevices = NBLK // BLK_DEV
    limits = jax.random.randint(first, (ndevices,), 250, 1001)
    draws = jax.random.randint(second, (STEPS, NBLK), 0, 1000)
    return (draws < jnp.repeat(limits, BLK_DEV)[None, :]).astype(jnp.int32)


def draw_boundary_cells(key, part):
    base = jax.random.fold_in(key, 303)
    first, second = jax.random.split(base)
    ndevices = NBLK // BLK_DEV
    keys = jax.random.split(first, ndevices)
    chosen = jax.vmap(lambda single: jax.random.permutation(single, BLK_DEV)[:BND_DEV])(keys).astype(jnp.int32)
    inside = jax.random.randint(second, (ndevices, BND_DEV), 0, E)
    return (chosen * E + inside).reshape(-1).astype(jnp.int32)


def draw_moved_from(key, part):
    base = jax.random.fold_in(key, 404)
    first, second = jax.random.split(base)
    ndevices = NBLK // BLK_DEV
    share = BLK_DEV // ndevices
    primary = jax.random.permutation(first, ndevices).astype(jnp.int32)
    missing = jnp.roll(primary, 1)
    targets = jnp.arange(ndevices, dtype=jnp.int32)
    counts = share * (1 + (targets[None, :] == primary[:, None]).astype(jnp.int32) - (targets[None, :] == missing[:, None]).astype(jnp.int32))
    column_sums = jnp.cumsum(counts, axis=0)
    row_starts = jnp.cumsum(counts, axis=1) - counts
    keys = jax.random.split(second, ndevices)
    shuffled = jax.vmap(lambda single: jax.random.permutation(single, BLK_DEV))(keys).astype(jnp.int32)
    slots = jnp.arange(NBLK, dtype=jnp.int32)
    target = slots // BLK_DEV
    within = slots % BLK_DEV
    source = jnp.sum((column_sums[:, target].T <= within[:, None]).astype(jnp.int32), axis=1)
    start = column_sums[source, target] - counts[source, target]
    offset = within - start
    local = shuffled[source, row_starts[source, target] + offset]
    return (source * BLK_DEV + local).astype(jnp.int32)


def set_ends(result, own_key, low, top_value):
    longest = result.shape.index(max(result.shape))
    spots = []
    for shift in (0, 1):
        where = [jax.random.randint(jax.random.fold_in(own_key, axis), (), 0, length) for axis, length in enumerate(result.shape)]
        where[longest] = (where[longest] + shift) % result.shape[longest]
        spots.append(tuple(where))
    return result.at[spots[0]].set(low).at[spots[1]].set(top_value)


def levels(stream_key, extent, cuts, smallest, high):
    factor_of = 1.0
    for axis_at, blocks in cuts:
        steps = jax.random.uniform(jax.random.fold_in(jax.random.fold_in(stream_key, 6), axis_at), (blocks,), jnp.float32, smallest / len(cuts), high / len(cuts))
        factor_of = factor_of * jnp.repeat(jnp.exp(steps), extent[axis_at] // blocks).reshape((-1,) + (1,) * (len(extent) - 1 - axis_at))
    return factor_of


def noise(stream_key, shape, width, bound, pieces=(), kind=jnp.bfloat16):
    result = jax.random.normal(stream_key, shape, jnp.float32) * width
    if len(pieces) > 0:
        result = levels(stream_key, shape, pieces, -0.22, 0.18) * result
    return jnp.clip(result, min=-bound, max=bound).astype(kind)


def setup_inputs(seed: int = 0) -> dict:
    arg_keys = jax.random.split(jax.random.key(seed), 13)
    return {
        "elevation": noise(arg_keys[0], (NBLK, E), 1.0, 6.0, ((0, 32),), jnp.float32),
        "momentum": noise(arg_keys[1], (NBLK, 2, E), 1.0, 6.0, ((0, 32),), jnp.float32),
        "depth": jnp.clip(jnp.exp(math.log(1.5) - 1.60943787 * jax.random.uniform(arg_keys[2], (NBLK, E), jnp.float32) ** levels(arg_keys[2], (NBLK, E), ((0, 32),), -0.2, 0.2)), 0.3, 1.5),
        "drag": jnp.clip(jnp.exp(math.log(0.6) - 2.4849067 * jax.random.uniform(arg_keys[3], (NBLK, E), jnp.float32) ** levels(arg_keys[3], (NBLK, E), ((0, 32),), -0.2, 0.2)), 0.05, 0.6),
        "div_weight": noise(arg_keys[4], (5, 2, E, E), (40 * E) ** -0.5, 0.078125, (), jnp.float32),
        "grad_weight": noise(arg_keys[5], (5, E, 2 * E), (20 * E) ** -0.5, 0.125, (), jnp.float32),
        "neighbours": draw_neighbours(jax.random.fold_in(arg_keys[12], 71), 0),
        "wet": draw_wet(jax.random.fold_in(arg_keys[12], 71), 0),
        "boundary_cells": draw_boundary_cells(jax.random.fold_in(arg_keys[12], 71), 0),
        "boundary_source": set_ends(jax.random.randint(arg_keys[9], (NBND,), 0, NPAR), jax.random.fold_in(arg_keys[9], 1), 0, NPAR - 1).astype(jnp.int32),
        "series": noise(arg_keys[10], (STEPS, NPAR), 1.0, 6.0, ((1, 32),), jnp.float32),
        "moved_from": draw_moved_from(jax.random.fold_in(arg_keys[12], 71), 0),
    }


relax_rate = 0.5
highest = lax.Precision.HIGHEST


def reference(elevation, momentum, depth, drag, div_weight, grad_weight, neighbours, wet, boundary_cells, boundary_source, series, moved_from):
    div_matrix = div_weight.reshape(10 * E, E)
    grad_matrix = grad_weight.reshape(5 * E, 2 * E)
    entry_device = jnp.arange(NBND, dtype=jnp.int32) // BND_DEV
    global_cells = (entry_device * (BLK_DEV * E) + boundary_cells).astype(jnp.int32)
    devices = jnp.arange(N_DOM, dtype=jnp.int32)
    for step in range(STEPS):
        mask = wet[step].astype(jnp.float32)[:, None]
        flows = momentum

        def divergence(device):
            rows = lax.dynamic_slice_in_dim(neighbours, device * BLK_DEV, BLK_DEV, 0)
            own = lax.dynamic_slice_in_dim(flows, device * BLK_DEV, BLK_DEV, 0)
            stacked = jnp.concatenate([own[:, None], flows[rows]], axis=1).reshape(BLK_DEV, 10 * E)
            return jnp.dot(stacked, div_matrix, precision=highest, preferred_element_type=jnp.float32)

        div = lax.map(divergence, devices).reshape(NBLK, E)
        level = elevation - mask * div
        flat = level.reshape(-1)
        forcing = series[step][boundary_source]
        flat = flat.at[global_cells].add(relax_rate * (forcing - flat[global_cells]))
        level = flat.reshape(NBLK, E)

        def gradient(device):
            rows = lax.dynamic_slice_in_dim(neighbours, device * BLK_DEV, BLK_DEV, 0)
            own = lax.dynamic_slice_in_dim(level, device * BLK_DEV, BLK_DEV, 0)
            stacked = jnp.concatenate([own[:, None], level[rows]], axis=1).reshape(BLK_DEV, 5 * E)
            return jnp.dot(stacked, grad_matrix, precision=highest, preferred_element_type=jnp.float32)

        grad = lax.map(gradient, devices).reshape(NBLK, 2, E)
        momentum = mask[:, :, None] * (momentum - depth[:, None] * grad) / (1.0 + drag)[:, None]
        elevation = level
    return elevation[moved_from], momentum[moved_from]
```

```python
import functools

import jax
import jax.numpy as jnp
from jax import lax
from jax.experimental import pallas as pl
from jax.experimental.pallas import tpu as pltpu
from jax.sharding import PartitionSpec as P

MESH = pl.DeviceIdType.MESH
f32 = jnp.float32
bf16 = jnp.bfloat16
relax_rate = 0.5


def halves(x):
    hi = x.astype(bf16)
    return hi, (x - hi.astype(f32)).astype(bf16)


def mm(a, b):
    return jnp.dot(a, b, preferred_element_type=f32)


def mm3(hi, lo, w_hi, w_lo):
    return mm(hi, w_hi) + (mm(lo, w_hi) + mm(hi, w_lo))


def hot(cond):
    return jnp.where(cond, 1.0, 0.0).astype(f32)


def iota(shape, dim):
    return lax.broadcasted_iota(jnp.int32, shape, dim).astype(f32)


def kernel(
    n, slots,
    elev_ref, mom_ref, depth_ref, drag_ref, divw_ref, gradw_ref, nb_ref, wet_ref,
    cells_ref, source_ref, series_ref, moved_ref,
    level_out, flow_out,
    meta, gathered, x_ref, dw_hi, dw_lo, gw_hi, gw_lo, damp_ref, depth_p, near_ref,
    force_ref, relax_ref, div_send, div_recv, lev_send, lev_recv, pack, packed, landed,
    meta_ss, meta_rs, div_ss, div_rs, lev_ss, lev_rs, mig_ss, mig_rs,
):
    me = lax.axis_index("dom")
    up = lax.rem(me + 1, n)
    down = lax.rem(me + n - 1, n)
    steps, width = series_ref.shape
    blocks, cells = elev_ref.shape
    half = blocks // 2
    span = blocks // width

    barrier = pltpu.get_barrier_semaphore()

    def greet(i, _):
        pl.semaphore_signal(
            barrier, inc=1, device_id=(lax.rem(me + i, n),), device_id_type=MESH
        )
        return 0

    lax.fori_loop(1, n, greet, 0)

    moved = moved_ref[...].astype(f32)
    meta[...] = jnp.zeros_like(meta)
    meta[0:steps, :] = series_ref[...]
    for i in range(span):
        meta[steps + i : steps + i + 1, :] = moved[:, i * width : (i + 1) * width]
    gathered[pl.ds(me, 1)] = meta[...][None]

    pl.semaphore_wait(barrier, n - 1)

    def tile_copy(target, source):
        return pltpu.make_async_remote_copy(
            src_ref=meta,
            dst_ref=gathered.at[source],
            send_sem=meta_ss.at[target],
            recv_sem=meta_rs.at[source],
            device_id=(target,),
            device_id_type=MESH,
        )

    def send_tile(i, _):
        tile_copy(lax.rem(me + i, n), me).start()
        return 0

    lax.fori_loop(1, n, send_tile, 0)

    base = (me * blocks).astype(f32)
    square = (blocks, blocks)
    sub, lane = iota(square, 0), iota(square, 1)
    nb = nb_ref[...].astype(f32)
    nbl = nb - base
    lower_own = jnp.logical_and(nbl[2:3] >= 0.0, nbl[2:3] < float(blocks))
    key_row = jnp.where(lower_own, nb[3:4] + float(blocks), lane[0:1])
    key_col = jnp.sum(jnp.where(sub == lane, key_row, 0.0), axis=1, keepdims=True)
    pos_row = jnp.sum(hot(key_col < key_row), axis=0, keepdims=True)
    pos_col = jnp.sum(hot(key_row < key_col), axis=1, keepdims=True)
    order = hot(sub == pos_row)
    order16 = order.astype(bf16)

    def place(ids):
        return jnp.sum(jnp.where(sub[:, : ids.shape[1]] == ids, pos_col, 0.0), axis=0, keepdims=True)

    vertical = jnp.where(lower_own, nbl[2:3], nbl[3:4])
    for k, ids in enumerate((nbl[0:1], nbl[1:2], vertical)):
        col = jnp.sum(order * place(ids), axis=1, keepdims=True)
        near_ref[k * blocks : (k + 1) * blocks, :] = hot(lane == col).astype(bf16)

    field = jnp.concatenate(
        [
            mom_ref[pl.ds(0, blocks, 2), :],
            mom_ref[pl.ds(1, blocks, 2), :],
            elev_ref[...],
            depth_ref[...],
            drag_ref[...],
        ],
        axis=1,
    )
    hi, lo = halves(field)
    field = mm(order16, hi) + mm(order16, lo)
    x_ref[...] = field[:, : 2 * cells]
    elevation0 = field[:, 2 * cells : 3 * cells]
    depth_p[...] = field[:, 3 * cells : 4 * cells]
    damping = 1.0 / (1.0 + field[:, 4 * cells :])
    wet = wet_ref[...].astype(f32)
    for s in range(steps):
        mask = jnp.sum(order * wet[s : s + 1], axis=1, keepdims=True)
        damp_ref[s, :, :cells] = jnp.broadcast_to(mask, (blocks, cells))
        damp_ref[s, :, cells:] = mask * damping
    hi, lo = halves(divw_ref[...])
    dw_hi[...] = hi
    dw_lo[...] = lo
    hi, lo = halves(gradw_ref[...])
    gw_hi[...] = hi
    gw_lo[...] = lo

    def tile_done(i, _):
        source = lax.rem(me + i, n)
        tile_copy(source, source).wait_recv()
        return 0

    lax.fori_loop(1, n, tile_done, 0)
    tall = meta.shape[0]
    entries = cells_ref.shape[1]
    point = source_ref[...].astype(f32)
    chunk = jnp.floor((point + 0.5) * (1.0 / width))
    spot = point - chunk * width
    pick = hot(iota((width, entries), 0) == spot).astype(bf16)
    everyone = gathered[...]
    hi, lo = halves(everyone.reshape(n * tall, width))
    found = (mm(hi, pick) + mm(lo, pick)).reshape(n, tall, entries)
    found = jnp.sum(jnp.where(iota(found.shape, 0) == chunk[None], found, 0.0), axis=0)
    cell = cells_ref[...].astype(f32)
    block = jnp.floor((cell + 0.5) * (1.0 / cells))
    element = cell - block * cells
    block_place = jnp.sum(
        jnp.where(iota((blocks, entries), 0) == block, pos_col, 0.0), axis=0, keepdims=True
    )
    rows = hot(iota((blocks, entries), 0) == block_place).astype(bf16)
    columns = hot(iota((cells, entries), 0) == element)

    def spread(values):
        return lax.dot_general(
            rows, values, (((1,), (1,)), ((), ())), preferred_element_type=f32
        )

    relax_ref[...] = relax_rate * spread(columns.astype(bf16))
    for s in range(steps):
        hi, lo = halves(columns * found[s : s + 1])
        force_ref[s] = spread(hi) + spread(lo)

    takes = jnp.concatenate([everyone[:, steps + i, :] for i in range(span)], axis=1) - base
    mine = hot(jnp.logical_and(takes >= 0.0, takes < float(blocks)))
    rank = mm(mine.astype(bf16), hot(sub < lane).astype(bf16))
    rank = jnp.where(mine > 0.0, rank, -1.0)
    cube = (n, slots, blocks)
    chosen = jnp.where(rank[:, None, :] == iota(cube, 1), takes[:, None, :] + 1.0, 0.0)
    chosen = jnp.sum(chosen.reshape(n * slots, blocks), axis=1, keepdims=True) - 1.0
    lanes = iota((n * slots, blocks), 1)
    pack[...] = mm(hot(lanes == chosen).astype(bf16), hot(lane == pos_col).astype(bf16)).astype(bf16)

    def halo(send, recv, ss, rs, step, way):
        return pltpu.make_async_remote_copy(
            src_ref=send,
            dst_ref=recv.at[step, way],
            send_sem=ss.at[step, way],
            recv_sem=rs.at[step, way],
            device_id=((up, down)[way],),
            device_id_type=MESH,
        )

    def div_copy(step, way):
        return halo(div_send.at[step, way], div_recv, div_ss, div_rs, step, way)

    def lev_copy(step, way):
        rows_out = (pl.ds(half, half), pl.ds(0, half))[way]
        return halo(lev_send.at[step, rows_out], lev_recv, lev_ss, lev_rs, step, way)

    def sl(k, size):
        return slice(k * size, (k + 1) * size)

    wide = 2 * cells

    def one_step(step, elevation):
        x = x_ref[...]
        hi, lo = halves(x)
        for way, rows_out, slot in ((0, slice(half, blocks), 3), (1, slice(0, half), 4)):
            div_send[step, way] = mm3(
                hi[rows_out], lo[rows_out], dw_hi[sl(slot, wide), :], dw_lo[sl(slot, wide), :]
            )
            div_copy(step, way).start()
        near = mm(near_ref[...], jnp.concatenate([hi, lo], axis=1)).astype(bf16)
        three = slice(0, 3 * wide)
        hi3 = jnp.concatenate([hi, near[:blocks, :wide], near[blocks : 2 * blocks, :wide]], axis=1)
        lo3 = jnp.concatenate([lo, near[:blocks, wide:], near[blocks : 2 * blocks, wide:]], axis=1)
        div = mm3(hi3, lo3, dw_hi[three, :], dw_lo[three, :])
        upper = near[2 * blocks :]
        div = div + jnp.concatenate(
            [
                mm3(
                    upper[r, :wide], upper[r, wide:], dw_hi[sl(k, wide), :], dw_lo[sl(k, wide), :]
                )
                for r, k in ((slice(0, half), 4), (slice(half, blocks), 3))
            ],
            axis=0,
        )
        div_copy(step, 0).wait_recv()
        div_copy(step, 1).wait_recv()
        div = div + jnp.concatenate([div_recv[step, 0], div_recv[step, 1]], axis=0)
        level = elevation - damp_ref[step, :, :cells] * div
        level = level + relax_ref[...] * (force_ref[step] - level)
        lev_send[step] = level
        lev_copy(step, 0).start()
        lev_copy(step, 1).start()
        hi, lo = halves(level)
        near = mm(near_ref[...], jnp.concatenate([hi, lo], axis=1)).astype(bf16)
        three = slice(0, 3 * cells)
        hi3 = jnp.concatenate([hi, near[:blocks, :cells], near[blocks : 2 * blocks, :cells]], axis=1)
        lo3 = jnp.concatenate([lo, near[:blocks, cells:], near[blocks : 2 * blocks, cells:]], axis=1)
        grad = mm3(hi3, lo3, gw_hi[three, :], gw_lo[three, :])
        upper = near[2 * blocks :]
        grad = grad + jnp.concatenate(
            [
                mm3(
                    upper[r, :cells], upper[r, cells:],
                    gw_hi[sl(k, cells), :], gw_lo[sl(k, cells), :],
                )
                for r, k in ((slice(0, half), 4), (slice(half, blocks), 3))
            ],
            axis=0,
        )
        lev_copy(step, 0).wait_recv()
        lev_copy(step, 1).wait_recv()
        away = [
            mm3(*halves(lev_recv[step, way]), gw_hi[sl(k, cells), :], gw_lo[sl(k, cells), :])
            for way, k in ((0, 3), (1, 4))
        ]
        grad = grad + jnp.concatenate(away, axis=0)
        depth = depth_p[...]
        damp = damp_ref[step, :, cells:]
        x_ref[:, :cells] = damp * (x[:, :cells] - depth * grad[:, :cells])
        x_ref[:, cells:] = damp * (x[:, cells:] - depth * grad[:, cells:])
        return level

    level = lax.fori_loop(0, steps, one_step, elevation0)

    state = jnp.concatenate([level, x_ref[...]], axis=1)
    hi, lo = halves(state)
    moving = mm(pack[...], hi) + mm(pack[...], lo)
    packed[...] = moving.reshape(packed.shape)
    landed[pl.ds(me, 1)] = packed[pl.ds(me, 1)]

    def state_copy(target, source):
        return pltpu.make_async_remote_copy(
            src_ref=packed.at[target],
            dst_ref=landed.at[source],
            send_sem=mig_ss.at[target],
            recv_sem=mig_rs.at[source],
            device_id=(target,),
            device_id_type=MESH,
        )

    def send_state(i, _):
        state_copy(lax.rem(me + i, n), me).start()
        return 0

    lax.fori_loop(1, n, send_state, 0)

    owner_row = jnp.floor((moved + 0.5) * (1.0 / blocks))
    owner_col = jnp.sum(jnp.where(sub == lane, owner_row, 0.0), axis=1, keepdims=True)
    ahead = jnp.sum(
        jnp.where(lane < sub, hot(owner_row == owner_col), 0.0), axis=1, keepdims=True
    )
    where_from = owner_col * float(slots) + ahead
    unpack = hot(iota((blocks, n * slots), 1) == where_from).astype(bf16)

    def state_done(i, _):
        source = lax.rem(me + i, n)
        state_copy(source, source).wait_recv()
        return 0

    lax.fori_loop(1, n, state_done, 0)
    hi, lo = halves(landed[...].reshape(n * slots, 3 * cells))
    result = mm(unpack, hi) + mm(unpack, lo)
    level_out[...] = result[:, :cells]
    flow_out[pl.ds(0, blocks, 2), :] = result[:, cells : 2 * cells]
    flow_out[pl.ds(1, blocks, 2), :] = result[:, 2 * cells :]

    def sent(i, _):
        target = lax.rem(me + i, n)
        tile_copy(target, me).wait_send()
        state_copy(target, me).wait_send()
        return 0

    lax.fori_loop(1, n, sent, 0)

    def halo_sent(step, _):
        for way in (0, 1):
            div_copy(step, way).wait_send()
            lev_copy(step, way).wait_send()
        return 0

    lax.fori_loop(0, steps, halo_sent, 0)


def local(
    n,
    elevation,
    momentum,
    depth,
    drag,
    div_weight,
    grad_weight,
    neighbours,
    wet,
    boundary_cells,
    boundary_source,
    series,
    moved_from,
):
    blocks, cells = elevation.shape
    steps, width = series.shape
    half = blocks // 2
    wide = 2 * cells
    portion = 2 * blocks // n
    slots = -(-portion // 8) * 8
    tall = -(-(steps + blocks // width) // 8) * 8
    vmem, dma = pltpu.VMEM, pltpu.SemaphoreType.DMA
    level, flow = pl.pallas_call(
        functools.partial(kernel, n, slots),
        out_shape=(
            jax.ShapeDtypeStruct((blocks, cells), f32),
            jax.ShapeDtypeStruct((2 * blocks, cells), f32),
        ),
        in_specs=[pl.BlockSpec(memory_space=vmem)] * 12,
        out_specs=(pl.BlockSpec(memory_space=vmem),) * 2,
        scratch_shapes=[
            vmem((tall, width), f32),
            vmem((n, tall, width), f32),
            vmem((blocks, wide), f32),
            vmem((5 * wide, cells), bf16),
            vmem((5 * wide, cells), bf16),
            vmem((5 * cells, wide), bf16),
            vmem((5 * cells, wide), bf16),
            vmem((steps, blocks, wide), f32),
            vmem((blocks, cells), f32),
            vmem((3 * blocks, blocks), bf16),
            vmem((steps, blocks, cells), f32),
            vmem((blocks, cells), f32),
            vmem((steps, 2, half, cells), f32),
            vmem((steps, 2, half, cells), f32),
            vmem((steps, blocks, cells), f32),
            vmem((steps, 2, half, cells), f32),
            vmem((n * slots, blocks), bf16),
            vmem((n, slots, 3 * cells), f32),
            vmem((n, slots, 3 * cells), f32),
            dma((n,)),
            dma((n,)),
            dma((steps, 2)),
            dma((steps, 2)),
            dma((steps, 2)),
            dma((steps, 2)),
            dma((n,)),
            dma((n,)),
        ],
        compiler_params=pltpu.CompilerParams(
            collective_id=0, has_side_effects=True, vmem_limit_bytes=48 * 1024 * 1024
        ),
        name="surge",
    )(
        elevation,
        momentum.reshape(2 * blocks, cells),
        depth,
        drag,
        div_weight.reshape(5 * wide, cells),
        grad_weight.reshape(5 * cells, wide),
        neighbours.T,
        wet,
        boundary_cells.reshape(1, -1),
        boundary_source.reshape(1, -1),
        series,
        moved_from.reshape(1, -1),
    )
    return level, flow.reshape(blocks, 2, cells)


def solution(mesh):
    n = mesh.shape["dom"]
    return jax.shard_map(
        functools.partial(local, n),
        mesh=mesh,
        in_specs=(
            P("dom", None),
            P("dom", None, None),
            P("dom", None),
            P("dom", None),
            P(),
            P(),
            P("dom", None),
            P(None, "dom"),
            P("dom"),
            P("dom"),
            P(None, "dom"),
            P("dom"),
        ),
        out_specs=(P("dom", None), P("dom", None, None)),
        check_vma=False,
    )
```

```python
import functools

import jax
import jax.numpy as jnp
from jax import lax
from jax.experimental import pallas as pl
from jax.experimental.pallas import tpu as pltpu
from jax.sharding import PartitionSpec as P

MESH = pl.DeviceIdType.MESH
f32 = jnp.float32
bf16 = jnp.bfloat16
relax_rate = 0.5


def halves(x):
    hi = x.astype(bf16)
    return hi, (x - hi.astype(f32)).astype(bf16)


def mm(a, b):
    return jnp.dot(a, b, preferred_element_type=f32)


def mm3(hi, lo, w_hi, w_lo):
    return mm(hi, w_hi) + (mm(lo, w_hi) + mm(hi, w_lo))


def hot(cond):
    return jnp.where(cond, 1.0, 0.0).astype(f32)


def iota(shape, dim):
    return lax.broadcasted_iota(jnp.int32, shape, dim).astype(f32)


def kernel(
    n, slots,
    elev_hbm, mom_hbm, depth_hbm, drag_hbm, divw_hbm, gradw_hbm, nb_hbm, wet_hbm,
    cells_hbm, source_hbm, series_hbm, moved_hbm,
    level_out, flow_out,
    elev_ref, mom_ref, depth_ref, drag_ref, divw_ref, gradw_ref, nb_ref, wet_ref,
    cells_ref, source_ref, series_ref, moved_ref,
    meta, gathered, x_ref, dw_hi, dw_lo, gw_hi, gw_lo, damp_ref, depth_p, near_ref,
    force_ref, relax_ref, div_send, div_recv, lev_send, lev_recv, pack, packed, landed,
    in_ss, meta_ss, meta_rs, div_ss, div_rs, lev_ss, lev_rs, mig_ss, mig_rs,
):
    me = lax.axis_index("dom")
    up = lax.rem(me + 1, n)
    down = lax.rem(me + n - 1, n)
    steps, width = series_ref.shape
    blocks, cells = elev_ref.shape
    half = blocks // 2
    wide = 2 * cells
    span = blocks // width

    inputs = [
        pltpu.make_async_copy(src, dst, in_ss.at[i])
        for i, (src, dst) in enumerate(
            (
                (nb_hbm, nb_ref),
                (moved_hbm, moved_ref),
                (series_hbm, series_ref),
                (wet_hbm, wet_ref),
                (cells_hbm, cells_ref),
                (source_hbm, source_ref),
                (mom_hbm, mom_ref),
                (elev_hbm, elev_ref),
                (depth_hbm, depth_ref),
                (drag_hbm, drag_ref),
                (divw_hbm, divw_ref),
                (gradw_hbm, gradw_ref),
            )
        )
    ]
    for copy in inputs:
        copy.start()

    barrier = pltpu.get_barrier_semaphore()

    def greet(i, _):
        pl.semaphore_signal(
            barrier, inc=1, device_id=(lax.rem(me + i, n),), device_id_type=MESH
        )
        return 0

    lax.fori_loop(1, n, greet, 0)

    def partner(i):
        j = i - 1
        return lax.rem(me + (j + 1) // 2 + (1 - j % 2) * (n // 2), n)

    def sl(k, size):
        return slice(k * size, (k + 1) * size)

    for copy in inputs[:6]:
        copy.wait()
    base = (me * blocks).astype(f32)
    square = (blocks, blocks)
    sub, lane = iota(square, 0), iota(square, 1)
    nb = nb_ref[...].astype(f32)
    nbl = nb - base
    lower_own = jnp.logical_and(nbl[2:3] >= 0.0, nbl[2:3] < float(blocks))
    key_row = jnp.where(lower_own, nb[3:4] + float(blocks), lane[0:1])
    key_col = jnp.sum(jnp.where(sub == lane, key_row, 0.0), axis=1, keepdims=True)
    pos_row = jnp.sum(hot(key_col < key_row), axis=0, keepdims=True)
    pos_col = jnp.sum(hot(key_row < key_col), axis=1, keepdims=True)
    order = hot(sub == pos_row)
    order16 = order.astype(bf16)

    for copy in inputs[6:10]:
        copy.wait()
    field = jnp.concatenate(
        [
            mom_ref[pl.ds(0, blocks, 2), :],
            mom_ref[pl.ds(1, blocks, 2), :],
            elev_ref[...],
            depth_ref[...],
            drag_ref[...],
        ],
        axis=1,
    )
    hi, lo = halves(field)
    field = mm(order16, hi) + mm(order16, lo)
    x_ref[...] = field[:, :wide]
    elevation0 = field[:, wide : 3 * cells]
    depth_p[...] = field[:, 3 * cells : 4 * cells]
    damping = 1.0 / (1.0 + field[:, 4 * cells :])
    inputs[10].wait()
    hi, lo = halves(divw_ref[...])
    dw_hi[...] = hi
    dw_lo[...] = lo

    def halo(send, recv, ss, rs, step, way):
        return pltpu.make_async_remote_copy(
            src_ref=send,
            dst_ref=recv.at[step, way],
            send_sem=ss.at[step, way],
            recv_sem=rs.at[step, way],
            device_id=((up, down)[way],),
            device_id_type=MESH,
        )

    def div_copy(step, way):
        return halo(div_send.at[step, way], div_recv, div_ss, div_rs, step, way)

    def lev_copy(step, way):
        rows_out = (pl.ds(half, half), pl.ds(0, half))[way]
        return halo(lev_send.at[step, rows_out], lev_recv, lev_ss, lev_rs, step, way)

    def tile_copy(target, source):
        return pltpu.make_async_remote_copy(
            src_ref=meta,
            dst_ref=gathered.at[source],
            send_sem=meta_ss.at[target],
            recv_sem=meta_rs.at[source],
            device_id=(target,),
            device_id_type=MESH,
        )

    def state_copy(target, source):
        return pltpu.make_async_remote_copy(
            src_ref=packed.at[target],
            dst_ref=landed.at[source],
            send_sem=mig_ss.at[target],
            recv_sem=mig_rs.at[source],
            device_id=(target,),
            device_id_type=MESH,
        )

    moved = moved_ref[...].astype(f32)

    def open_up():
        meta[...] = jnp.zeros_like(meta)
        meta[0:steps, :] = series_ref[...]
        for i in range(span):
            meta[steps + i : steps + i + 1, :] = moved[:, i * width : (i + 1) * width]
        gathered[pl.ds(me, 1)] = meta[...][None]
        pl.semaphore_wait(barrier, n - 1)

    def send_tiles():
        def send(i, _):
            tile_copy(partner(i), me).start()
            return 0

        lax.fori_loop(1, n, send, 0)

        def place(ids):
            return jnp.sum(jnp.where(sub == ids, pos_col, 0.0), axis=0, keepdims=True)

        vertical = jnp.where(lower_own, nbl[2:3], nbl[3:4])
        for k, ids in enumerate((nbl[0:1], nbl[1:2], vertical)):
            col = jnp.sum(order * place(ids), axis=1, keepdims=True)
            near_ref[sl(k, blocks), :] = hot(lane == col).astype(bf16)
        wet = wet_ref[...].astype(f32)
        for s in range(steps):
            mask = jnp.sum(order * wet[s : s + 1], axis=1, keepdims=True)
            damp_ref[s, :, :cells] = jnp.broadcast_to(mask, (blocks, cells))
            damp_ref[s, :, cells:] = mask * damping

    def boundary():
        entries = cells_ref.shape[1]
        point = source_ref[...].astype(f32)
        chunk = jnp.floor((point + 0.5) * (1.0 / width))
        spot = point - chunk * width
        pick = hot(iota((width, entries), 0) == spot).astype(bf16)
        cell = cells_ref[...].astype(f32)
        block = jnp.floor((cell + 0.5) * (1.0 / cells))
        element = cell - block * cells
        block_place = jnp.sum(
            jnp.where(iota((blocks, entries), 0) == block, pos_col, 0.0), axis=0, keepdims=True
        )
        rows = hot(iota((blocks, entries), 0) == block_place).astype(bf16)
        columns = hot(iota((cells, entries), 0) == element)

        def spread(values):
            return lax.dot_general(
                rows, values, (((1,), (1,)), ((), ())), preferred_element_type=f32
            )

        relax_ref[...] = relax_rate * spread(columns.astype(bf16))

        def tile_done(i, _):
            source = lax.rem(me + i, n)
            tile_copy(source, source).wait_recv()
            return 0

        lax.fori_loop(1, n, tile_done, 0)
        tall = meta.shape[0]
        hi, lo = halves(gathered[...].reshape(n * tall, width))
        found = (mm(hi, pick) + mm(lo, pick)).reshape(n, tall, entries)
        found = jnp.sum(jnp.where(iota(found.shape, 0) == chunk[None], found, 0.0), axis=0)
        for s in range(steps):
            hi, lo = halves(columns * found[s : s + 1])
            force_ref[s] = spread(hi) + spread(lo)

    def choose():
        everyone = gathered[...]
        takes = jnp.concatenate([everyone[:, steps + i, :] for i in range(span)], axis=1) - base
        mine = hot(jnp.logical_and(takes >= 0.0, takes < float(blocks)))
        rank = mm(mine.astype(bf16), hot(sub < lane).astype(bf16))
        rank = jnp.where(mine > 0.0, rank, -1.0)
        cube = (n, slots, blocks)
        chosen = jnp.where(rank[:, None, :] == iota(cube, 1), takes[:, None, :] + 1.0, 0.0)
        chosen = jnp.sum(chosen.reshape(n * slots, blocks), axis=1, keepdims=True) - 1.0
        lanes = iota((n * slots, blocks), 1)
        pack[...] = mm(
            hot(lanes == chosen).astype(bf16), hot(lane == pos_col).astype(bf16)
        ).astype(bf16)

    def one_step(step, elevation, opening):
        x = x_ref[...]
        hi, lo = halves(x)
        for way, rows_out, slot in ((0, slice(half, blocks), 3), (1, slice(0, half), 4)):
            div_send[step, way] = mm3(
                hi[rows_out], lo[rows_out], dw_hi[sl(slot, wide), :], dw_lo[sl(slot, wide), :]
            )
            if not opening:
                div_copy(step, way).start()
        if opening:
            open_up()
            for way in (0, 1):
                div_copy(step, way).start()
            send_tiles()
        near = mm(near_ref[...], jnp.concatenate([hi, lo], axis=1)).astype(bf16)
        three = slice(0, 3 * wide)
        hi3 = jnp.concatenate([hi, near[:blocks, :wide], near[blocks : 2 * blocks, :wide]], axis=1)
        lo3 = jnp.concatenate([lo, near[:blocks, wide:], near[blocks : 2 * blocks, wide:]], axis=1)
        div = mm3(hi3, lo3, dw_hi[three, :], dw_lo[three, :])
        upper = near[2 * blocks :]
        div = div + jnp.concatenate(
            [
                mm3(
                    upper[r, :wide], upper[r, wide:], dw_hi[sl(k, wide), :], dw_lo[sl(k, wide), :]
                )
                for r, k in ((slice(0, half), 4), (slice(half, blocks), 3))
            ],
            axis=0,
        )
        if opening:
            boundary()
        div_copy(step, 0).wait_recv()
        div_copy(step, 1).wait_recv()
        div = div + jnp.concatenate([div_recv[step, 0], div_recv[step, 1]], axis=0)
        level = elevation - damp_ref[step, :, :cells] * div
        level = level + relax_ref[...] * (force_ref[step] - level)
        lev_send[step] = level
        lev_copy(step, 0).start()
        lev_copy(step, 1).start()
        if opening:
            inputs[11].wait()
            hi, lo = halves(gradw_ref[...])
            gw_hi[...] = hi
            gw_lo[...] = lo
        hi, lo = halves(level)
        near = mm(near_ref[...], jnp.concatenate([hi, lo], axis=1)).astype(bf16)
        three = slice(0, 3 * cells)
        hi3 = jnp.concatenate([hi, near[:blocks, :cells], near[blocks : 2 * blocks, :cells]], axis=1)
        lo3 = jnp.concatenate([lo, near[:blocks, cells:], near[blocks : 2 * blocks, cells:]], axis=1)
        grad = mm3(hi3, lo3, gw_hi[three, :], gw_lo[three, :])
        upper = near[2 * blocks :]
        grad = grad + jnp.concatenate(
            [
                mm3(
                    upper[r, :cells], upper[r, cells:],
                    gw_hi[sl(k, cells), :], gw_lo[sl(k, cells), :],
                )
                for r, k in ((slice(0, half), 4), (slice(half, blocks), 3))
            ],
            axis=0,
        )
        if opening:
            choose()
        lev_copy(step, 0).wait_recv()
        lev_copy(step, 1).wait_recv()
        away = [
            mm3(*halves(lev_recv[step, way]), gw_hi[sl(k, cells), :], gw_lo[sl(k, cells), :])
            for way, k in ((0, 3), (1, 4))
        ]
        grad = grad + jnp.concatenate(away, axis=0)
        depth = depth_p[...]
        damp = damp_ref[step, :, cells:]
        x_ref[:, :cells] = damp * (x[:, :cells] - depth * grad[:, :cells])
        x_ref[:, cells:] = damp * (x[:, cells:] - depth * grad[:, cells:])
        return level

    level = one_step(0, elevation0, True)
    level = lax.fori_loop(1, steps, lambda s, e: one_step(s, e, False), level)

    state = jnp.concatenate([level, x_ref[...]], axis=1)
    hi, lo = halves(state)
    moving = mm(pack[...], hi) + mm(pack[...], lo)
    packed[...] = moving.reshape(packed.shape)
    landed[pl.ds(me, 1)] = packed[pl.ds(me, 1)]

    def send_state(i, _):
        state_copy(partner(i), me).start()
        return 0

    lax.fori_loop(1, n, send_state, 0)

    owner_row = jnp.floor((moved + 0.5) * (1.0 / blocks))
    owner_col = jnp.sum(jnp.where(sub == lane, owner_row, 0.0), axis=1, keepdims=True)
    ahead = jnp.sum(
        jnp.where(lane < sub, hot(owner_row == owner_col), 0.0), axis=1, keepdims=True
    )
    where_from = owner_col * float(slots) + ahead
    unpack = hot(iota((blocks, n * slots), 1) == where_from).astype(bf16)

    def state_done(i, _):
        source = lax.rem(me + i, n)
        state_copy(source, source).wait_recv()
        return 0

    lax.fori_loop(1, n, state_done, 0)
    hi, lo = halves(landed[...].reshape(n * slots, 3 * cells))
    result = mm(unpack, hi) + mm(unpack, lo)
    level_out[...] = result[:, :cells]
    flow_out[pl.ds(0, blocks, 2), :] = result[:, cells : 2 * cells]
    flow_out[pl.ds(1, blocks, 2), :] = result[:, 2 * cells :]

    def sent(i, _):
        target = lax.rem(me + i, n)
        tile_copy(target, me).wait_send()
        state_copy(target, me).wait_send()
        return 0

    lax.fori_loop(1, n, sent, 0)

    def halo_sent(step, _):
        for way in (0, 1):
            div_copy(step, way).wait_send()
            lev_copy(step, way).wait_send()
        return 0

    lax.fori_loop(0, steps, halo_sent, 0)


def local(
    n,
    elevation,
    momentum,
    depth,
    drag,
    div_weight,
    grad_weight,
    neighbours,
    wet,
    boundary_cells,
    boundary_source,
    series,
    moved_from,
):
    blocks, cells = elevation.shape
    steps, width = series.shape
    half = blocks // 2
    wide = 2 * cells
    portion = 2 * blocks // n
    slots = -(-portion // 8) * 8
    tall = -(-(steps + blocks // width) // 8) * 8
    vmem, dma = pltpu.VMEM, pltpu.SemaphoreType.DMA
    level, flow = pl.pallas_call(
        functools.partial(kernel, n, slots),
        out_shape=(
            jax.ShapeDtypeStruct((blocks, cells), f32),
            jax.ShapeDtypeStruct((2 * blocks, cells), f32),
        ),
        in_specs=[pl.BlockSpec(memory_space=pl.ANY)] * 12,
        out_specs=(pl.BlockSpec(memory_space=vmem),) * 2,
        scratch_shapes=[
            vmem((blocks, cells), f32),
            vmem((2 * blocks, cells), f32),
            vmem((blocks, cells), f32),
            vmem((blocks, cells), f32),
            vmem((5 * wide, cells), f32),
            vmem((5 * cells, wide), f32),
            vmem((4, blocks), jnp.int32),
            vmem(wet.shape, jnp.int32),
            vmem((1, boundary_cells.shape[0]), jnp.int32),
            vmem((1, boundary_source.shape[0]), jnp.int32),
            vmem(series.shape, f32),
            vmem((1, blocks), jnp.int32),
            vmem((tall, width), f32),
            vmem((n, tall, width), f32),
            vmem((blocks, wide), f32),
            vmem((5 * wide, cells), bf16),
            vmem((5 * wide, cells), bf16),
            vmem((5 * cells, wide), bf16),
            vmem((5 * cells, wide), bf16),
            vmem((steps, blocks, wide), f32),
            vmem((blocks, cells), f32),
            vmem((3 * blocks, blocks), bf16),
            vmem((steps, blocks, cells), f32),
            vmem((blocks, cells), f32),
            vmem((steps, 2, half, cells), f32),
            vmem((steps, 2, half, cells), f32),
            vmem((steps, blocks, cells), f32),
            vmem((steps, 2, half, cells), f32),
            vmem((n * slots, blocks), bf16),
            vmem((n, slots, 3 * cells), f32),
            vmem((n, slots, 3 * cells), f32),
            dma((12,)),
            dma((n,)),
            dma((n,)),
            dma((steps, 2)),
            dma((steps, 2)),
            dma((steps, 2)),
            dma((steps, 2)),
            dma((n,)),
            dma((n,)),
        ],
        compiler_params=pltpu.CompilerParams(
            collective_id=0, has_side_effects=True, vmem_limit_bytes=60 * 1024 * 1024
        ),
        name="surge",
    )(
        elevation,
        momentum.reshape(2 * blocks, cells),
        depth,
        drag,
        div_weight.reshape(5 * wide, cells),
        grad_weight.reshape(5 * cells, wide),
        neighbours.T,
        wet,
        boundary_cells.reshape(1, -1),
        boundary_source.reshape(1, -1),
        series,
        moved_from.reshape(1, -1),
    )
    return level, flow.reshape(blocks, 2, cells)


def solution(mesh):
    n = mesh.shape["dom"]
    return jax.shard_map(
        functools.partial(local, n),
        mesh=mesh,
        in_specs=(
            P("dom", None),
            P("dom", None, None),
            P("dom", None),
            P("dom", None),
            P(),
            P(),
            P("dom", None),
            P(None, "dom"),
            P("dom"),
            P("dom"),
            P(None, "dom"),
            P("dom"),
        ),
        out_specs=(P("dom", None), P("dom", None, None)),
        check_vma=False,
    )
```

```python
import functools

import jax
import jax.numpy as jnp
from jax import lax
from jax.experimental import pallas as pl
from jax.experimental.pallas import tpu as pltpu
from jax.sharding import PartitionSpec as P

MESH = pl.DeviceIdType.MESH
f32 = jnp.float32
bf16 = jnp.bfloat16
relax_rate = 0.5


def halves(x):
    hi = x.astype(bf16)
    return hi, (x - hi.astype(f32)).astype(bf16)


def mm(a, b):
    return jnp.dot(a, b, preferred_element_type=f32)


def mm3(hi, lo, w_hi, w_lo):
    return mm(hi, w_hi) + (mm(lo, w_hi) + mm(hi, w_lo))


def hot(cond):
    return jnp.where(cond, 1.0, 0.0).astype(f32)


def iota(shape, dim):
    return lax.broadcasted_iota(jnp.int32, shape, dim).astype(f32)


def kernel(
    n, slots,
    elev_hbm, mom_hbm, depth_hbm, drag_hbm, divw_hbm, gradw_hbm, nb_hbm, wet_hbm,
    cells_hbm, source_hbm, series_hbm, moved_hbm,
    landed_level, landed_flow,
    elev_ref, mom_ref, depth_ref, drag_ref, divw_ref, gradw_ref, nb_ref, wet_ref,
    cells_ref, source_ref, series_ref, moved_ref,
    meta, gathered, x_ref, dw_hi, dw_lo, gw_hi, gw_lo, damp_ref, depth_p, near_ref,
    force_ref, relax_ref, div_send, div_recv, lev_send, lev_recv, pack, packed_level, packed_flow,
    in_ss, meta_ss, meta_rs, div_ss, div_rs, lev_ss, lev_rs, mig_ss, mig_rs, own_ss,
):
    me = lax.axis_index("dom")
    up = lax.rem(me + 1, n)
    down = lax.rem(me + n - 1, n)
    steps, width = series_ref.shape
    blocks, cells = elev_ref.shape
    half = blocks // 2
    wide = 2 * cells
    span = blocks // width

    inputs = [
        pltpu.make_async_copy(src, dst, in_ss.at[i])
        for i, (src, dst) in enumerate(
            (
                (nb_hbm, nb_ref),
                (moved_hbm, moved_ref),
                (series_hbm, series_ref),
                (wet_hbm, wet_ref),
                (cells_hbm, cells_ref),
                (source_hbm, source_ref),
                (mom_hbm, mom_ref),
                (elev_hbm, elev_ref),
                (depth_hbm, depth_ref),
                (drag_hbm, drag_ref),
                (divw_hbm, divw_ref),
                (gradw_hbm, gradw_ref),
            )
        )
    ]
    for copy in inputs:
        copy.start()

    barrier = pltpu.get_barrier_semaphore()

    def greet(i, _):
        pl.semaphore_signal(
            barrier, inc=1, device_id=(lax.rem(me + i, n),), device_id_type=MESH
        )
        return 0

    lax.fori_loop(1, n, greet, 0)

    def partner(i):
        j = i - 1
        return lax.rem(me + (j + 1) // 2 + (1 - j % 2) * (n // 2), n)

    def sl(k, size):
        return slice(k * size, (k + 1) * size)

    for copy in inputs[:6]:
        copy.wait()
    base = (me * blocks).astype(f32)
    square = (blocks, blocks)
    sub, lane = iota(square, 0), iota(square, 1)
    nb = nb_ref[...].astype(f32)
    nbl = nb - base
    lower_own = jnp.logical_and(nbl[2:3] >= 0.0, nbl[2:3] < float(blocks))
    key_row = jnp.where(lower_own, nb[3:4] + float(blocks), lane[0:1])
    key_col = jnp.sum(jnp.where(sub == lane, key_row, 0.0), axis=1, keepdims=True)
    pos_row = jnp.sum(hot(key_col < key_row), axis=0, keepdims=True)
    pos_col = jnp.sum(hot(key_row < key_col), axis=1, keepdims=True)
    order = hot(sub == pos_row)
    order16 = order.astype(bf16)

    for copy in inputs[6:10]:
        copy.wait()
    field = jnp.concatenate(
        [
            mom_ref[pl.ds(0, blocks, 2), :],
            mom_ref[pl.ds(1, blocks, 2), :],
            elev_ref[...],
            depth_ref[...],
            drag_ref[...],
        ],
        axis=1,
    )
    hi, lo = halves(field)
    field = mm(order16, hi) + mm(order16, lo)
    x_ref[...] = field[:, :wide]
    elevation0 = field[:, wide : 3 * cells]
    depth_p[...] = field[:, 3 * cells : 4 * cells]
    damping = 1.0 / (1.0 + field[:, 4 * cells :])
    inputs[10].wait()
    hi, lo = halves(divw_ref[...])
    dw_hi[...] = hi
    dw_lo[...] = lo

    def halo(send, recv, ss, rs, step, way):
        return pltpu.make_async_remote_copy(
            src_ref=send,
            dst_ref=recv.at[step, way],
            send_sem=ss.at[step, way],
            recv_sem=rs.at[step, way],
            device_id=((up, down)[way],),
            device_id_type=MESH,
        )

    def div_copy(step, way):
        return halo(div_send.at[step, way], div_recv, div_ss, div_rs, step, way)

    def lev_copy(step, way):
        rows_out = (pl.ds(half, half), pl.ds(0, half))[way]
        return halo(lev_send.at[step, rows_out], lev_recv, lev_ss, lev_rs, step, way)

    def tile_copy(target, source):
        return pltpu.make_async_remote_copy(
            src_ref=meta,
            dst_ref=gathered.at[source],
            send_sem=meta_ss.at[target],
            recv_sem=meta_rs.at[source],
            device_id=(target,),
            device_id_type=MESH,
        )

    def state_copy(kind, target, source):
        src, dst = ((packed_level, landed_level), (packed_flow, landed_flow))[kind]
        return pltpu.make_async_remote_copy(
            src_ref=src.at[target],
            dst_ref=dst.at[source],
            send_sem=mig_ss.at[kind, target],
            recv_sem=mig_rs.at[kind, source],
            device_id=(target,),
            device_id_type=MESH,
        )

    def own_copy(kind):
        src, dst = ((packed_level, landed_level), (packed_flow, landed_flow))[kind]
        return pltpu.make_async_copy(src.at[me], dst.at[me], own_ss.at[kind])

    def migrate(kind, hi, lo):
        src = (packed_level, packed_flow)[kind]
        src[...] = (mm(pack[...], hi) + mm(pack[...], lo)).reshape(src.shape)

        def send(i, _):
            state_copy(kind, partner(i), me).start()
            return 0

        lax.fori_loop(1, n, send, 0)
        own_copy(kind).start()

    moved = moved_ref[...].astype(f32)

    def open_up():
        meta[...] = jnp.zeros_like(meta)
        meta[0:steps, :] = series_ref[...]
        for i in range(span):
            meta[steps + i : steps + i + 1, :] = moved[:, i * width : (i + 1) * width]
        gathered[pl.ds(me, 1)] = meta[...][None]
        pl.semaphore_wait(barrier, n - 1)

    def send_tiles():
        def send(i, _):
            tile_copy(partner(i), me).start()
            return 0

        lax.fori_loop(1, n, send, 0)

        def place(ids):
            return jnp.sum(jnp.where(sub == ids, pos_col, 0.0), axis=0, keepdims=True)

        vertical = jnp.where(lower_own, nbl[2:3], nbl[3:4])
        for k, ids in enumerate((nbl[0:1], nbl[1:2], vertical)):
            col = jnp.sum(order * place(ids), axis=1, keepdims=True)
            near_ref[sl(k, blocks), :] = hot(lane == col).astype(bf16)
        wet = wet_ref[...].astype(f32)
        for s in range(steps):
            mask = jnp.sum(order * wet[s : s + 1], axis=1, keepdims=True)
            damp_ref[s, :, :cells] = jnp.broadcast_to(mask, (blocks, cells))
            damp_ref[s, :, cells:] = mask * damping

    def boundary():
        entries = cells_ref.shape[1]
        point = source_ref[...].astype(f32)
        chunk = jnp.floor((point + 0.5) * (1.0 / width))
        spot = point - chunk * width
        pick = hot(iota((width, entries), 0) == spot).astype(bf16)
        cell = cells_ref[...].astype(f32)
        block = jnp.floor((cell + 0.5) * (1.0 / cells))
        element = cell - block * cells
        block_place = jnp.sum(
            jnp.where(iota((blocks, entries), 0) == block, pos_col, 0.0), axis=0, keepdims=True
        )
        rows = hot(iota((blocks, entries), 0) == block_place).astype(bf16)
        columns = hot(iota((cells, entries), 0) == element)

        def spread(values):
            return lax.dot_general(
                rows, values, (((1,), (1,)), ((), ())), preferred_element_type=f32
            )

        relax_ref[...] = relax_rate * spread(columns.astype(bf16))

        def tile_done(i, _):
            source = lax.rem(me + i, n)
            tile_copy(source, source).wait_recv()
            return 0

        lax.fori_loop(1, n, tile_done, 0)
        tall = meta.shape[0]
        hi, lo = halves(gathered[...].reshape(n * tall, width))
        found = (mm(hi, pick) + mm(lo, pick)).reshape(n, tall, entries)
        found = jnp.sum(jnp.where(iota(found.shape, 0) == chunk[None], found, 0.0), axis=0)
        for s in range(steps):
            hi, lo = halves(columns * found[s : s + 1])
            force_ref[s] = spread(hi) + spread(lo)

    def choose():
        everyone = gathered[...]
        takes = jnp.concatenate([everyone[:, steps + i, :] for i in range(span)], axis=1) - base
        mine = hot(jnp.logical_and(takes >= 0.0, takes < float(blocks)))
        rank = mm(mine.astype(bf16), hot(sub < lane).astype(bf16))
        rank = jnp.where(mine > 0.0, rank, -1.0)
        cube = (n, slots, blocks)
        chosen = jnp.where(rank[:, None, :] == iota(cube, 1), takes[:, None, :] + 1.0, 0.0)
        chosen = jnp.sum(chosen.reshape(n * slots, blocks), axis=1, keepdims=True) - 1.0
        lanes = iota((n * slots, blocks), 1)
        pack[...] = mm(
            hot(lanes == chosen).astype(bf16), hot(lane == pos_col).astype(bf16)
        ).astype(bf16)

    def one_step(step, elevation, opening, closing):
        x = x_ref[...]
        hi, lo = halves(x)
        for way, rows_out, slot in ((0, slice(half, blocks), 3), (1, slice(0, half), 4)):
            div_send[step, way] = mm3(
                hi[rows_out], lo[rows_out], dw_hi[sl(slot, wide), :], dw_lo[sl(slot, wide), :]
            )
            if not opening:
                div_copy(step, way).start()
        if opening:
            open_up()
            for way in (0, 1):
                div_copy(step, way).start()
            send_tiles()
        near = mm(near_ref[...], jnp.concatenate([hi, lo], axis=1)).astype(bf16)
        three = slice(0, 3 * wide)
        hi3 = jnp.concatenate([hi, near[:blocks, :wide], near[blocks : 2 * blocks, :wide]], axis=1)
        lo3 = jnp.concatenate([lo, near[:blocks, wide:], near[blocks : 2 * blocks, wide:]], axis=1)
        div = mm3(hi3, lo3, dw_hi[three, :], dw_lo[three, :])
        upper = near[2 * blocks :]
        div = div + jnp.concatenate(
            [
                mm3(
                    upper[r, :wide], upper[r, wide:], dw_hi[sl(k, wide), :], dw_lo[sl(k, wide), :]
                )
                for r, k in ((slice(0, half), 4), (slice(half, blocks), 3))
            ],
            axis=0,
        )
        if opening:
            boundary()
        div_copy(step, 0).wait_recv()
        div_copy(step, 1).wait_recv()
        div = div + jnp.concatenate([div_recv[step, 0], div_recv[step, 1]], axis=0)
        level = elevation - damp_ref[step, :, :cells] * div
        level = level + relax_ref[...] * (force_ref[step] - level)
        lev_send[step] = level
        lev_copy(step, 0).start()
        lev_copy(step, 1).start()
        if opening:
            inputs[11].wait()
            hi, lo = halves(gradw_ref[...])
            gw_hi[...] = hi
            gw_lo[...] = lo
        hi, lo = halves(level)
        near = mm(near_ref[...], jnp.concatenate([hi, lo], axis=1)).astype(bf16)
        three = slice(0, 3 * cells)
        hi3 = jnp.concatenate([hi, near[:blocks, :cells], near[blocks : 2 * blocks, :cells]], axis=1)
        lo3 = jnp.concatenate([lo, near[:blocks, cells:], near[blocks : 2 * blocks, cells:]], axis=1)
        grad = mm3(hi3, lo3, gw_hi[three, :], gw_lo[three, :])
        upper = near[2 * blocks :]
        grad = grad + jnp.concatenate(
            [
                mm3(
                    upper[r, :cells], upper[r, cells:],
                    gw_hi[sl(k, cells), :], gw_lo[sl(k, cells), :],
                )
                for r, k in ((slice(0, half), 4), (slice(half, blocks), 3))
            ],
            axis=0,
        )
        if opening:
            choose()
        if closing:
            migrate(0, hi, lo)
        lev_copy(step, 0).wait_recv()
        lev_copy(step, 1).wait_recv()
        away = [
            mm3(*halves(lev_recv[step, way]), gw_hi[sl(k, cells), :], gw_lo[sl(k, cells), :])
            for way, k in ((0, 3), (1, 4))
        ]
        grad = grad + jnp.concatenate(away, axis=0)
        depth = depth_p[...]
        damp = damp_ref[step, :, cells:]
        x_ref[:, :cells] = damp * (x[:, :cells] - depth * grad[:, :cells])
        x_ref[:, cells:] = damp * (x[:, cells:] - depth * grad[:, cells:])
        return level

    level = one_step(0, elevation0, True, False)
    level = lax.fori_loop(1, steps - 1, lambda s, e: one_step(s, e, False, False), level)
    one_step(steps - 1, level, False, True)
    migrate(1, *halves(x_ref[...]))

    def arrived(i, _):
        source = lax.rem(me + i, n)
        for kind in (0, 1):
            state_copy(kind, source, source).wait_recv()
        return 0

    lax.fori_loop(1, n, arrived, 0)

    def sent(i, _):
        target = lax.rem(me + i, n)
        tile_copy(target, me).wait_send()
        for kind in (0, 1):
            state_copy(kind, target, me).wait_send()
        return 0

    lax.fori_loop(1, n, sent, 0)
    for kind in (0, 1):
        own_copy(kind).wait()

    def halo_sent(step, _):
        for way in (0, 1):
            div_copy(step, way).wait_send()
            lev_copy(step, way).wait_send()
        return 0

    lax.fori_loop(0, steps, halo_sent, 0)


def settle(slots, moved_ref, landed_level, landed_flow, level_out, flow_out):
    blocks, cells = level_out.shape
    places = landed_level.shape[0]
    square = (blocks, blocks)
    sub, lane = iota(square, 0), iota(square, 1)
    owner_row = jnp.floor((moved_ref[...].astype(f32) + 0.5) * (1.0 / blocks))
    owner_col = jnp.sum(jnp.where(sub == lane, owner_row, 0.0), axis=1, keepdims=True)
    ahead = jnp.sum(
        jnp.where(lane < sub, hot(owner_row == owner_col), 0.0), axis=1, keepdims=True
    )
    where_from = owner_col * float(slots) + ahead
    unpack = hot(iota((blocks, places), 1) == where_from).astype(bf16)
    hi, lo = halves(landed_level[...])
    level_out[...] = mm(unpack, hi) + mm(unpack, lo)
    hi, lo = halves(landed_flow[...])
    flow = mm(unpack, hi) + mm(unpack, lo)
    flow_out[pl.ds(0, blocks, 2), :] = flow[:, :cells]
    flow_out[pl.ds(1, blocks, 2), :] = flow[:, cells:]


def local(
    n,
    elevation,
    momentum,
    depth,
    drag,
    div_weight,
    grad_weight,
    neighbours,
    wet,
    boundary_cells,
    boundary_source,
    series,
    moved_from,
):
    blocks, cells = elevation.shape
    steps, width = series.shape
    half = blocks // 2
    wide = 2 * cells
    portion = 2 * blocks // n
    slots = -(-portion // 8) * 8
    tall = -(-(steps + blocks // width) // 8) * 8
    vmem, dma = pltpu.VMEM, pltpu.SemaphoreType.DMA
    landed_level, landed_flow = pl.pallas_call(
        functools.partial(kernel, n, slots),
        out_shape=(
            jax.ShapeDtypeStruct((n, slots, cells), f32),
            jax.ShapeDtypeStruct((n, slots, wide), f32),
        ),
        in_specs=[pl.BlockSpec(memory_space=pl.ANY)] * 12,
        out_specs=(pl.BlockSpec(memory_space=pl.ANY),) * 2,
        scratch_shapes=[
            vmem((blocks, cells), f32),
            vmem((2 * blocks, cells), f32),
            vmem((blocks, cells), f32),
            vmem((blocks, cells), f32),
            vmem((5 * wide, cells), f32),
            vmem((5 * cells, wide), f32),
            vmem((4, blocks), jnp.int32),
            vmem(wet.shape, jnp.int32),
            vmem((1, boundary_cells.shape[0]), jnp.int32),
            vmem((1, boundary_source.shape[0]), jnp.int32),
            vmem(series.shape, f32),
            vmem((1, blocks), jnp.int32),
            vmem((tall, width), f32),
            vmem((n, tall, width), f32),
            vmem((blocks, wide), f32),
            vmem((5 * wide, cells), bf16),
            vmem((5 * wide, cells), bf16),
            vmem((5 * cells, wide), bf16),
            vmem((5 * cells, wide), bf16),
            vmem((steps, blocks, wide), f32),
            vmem((blocks, cells), f32),
            vmem((3 * blocks, blocks), bf16),
            vmem((steps, blocks, cells), f32),
            vmem((blocks, cells), f32),
            vmem((steps, 2, half, cells), f32),
            vmem((steps, 2, half, cells), f32),
            vmem((steps, blocks, cells), f32),
            vmem((steps, 2, half, cells), f32),
            vmem((n * slots, blocks), bf16),
            vmem((n, slots, cells), f32),
            vmem((n, slots, wide), f32),
            dma((12,)),
            dma((n,)),
            dma((n,)),
            dma((steps, 2)),
            dma((steps, 2)),
            dma((steps, 2)),
            dma((steps, 2)),
            dma((2, n)),
            dma((2, n)),
            dma((2,)),
        ],
        compiler_params=pltpu.CompilerParams(
            collective_id=0, has_side_effects=True, vmem_limit_bytes=60 * 1024 * 1024
        ),
        name="surge",
    )(
        elevation,
        momentum.reshape(2 * blocks, cells),
        depth,
        drag,
        div_weight.reshape(5 * wide, cells),
        grad_weight.reshape(5 * cells, wide),
        neighbours.T,
        wet,
        boundary_cells.reshape(1, -1),
        boundary_source.reshape(1, -1),
        series,
        moved_from.reshape(1, -1),
    )
    level, flow = pl.pallas_call(
        functools.partial(settle, slots),
        out_shape=(
            jax.ShapeDtypeStruct((blocks, cells), f32),
            jax.ShapeDtypeStruct((2 * blocks, cells), f32),
        ),
        in_specs=[pl.BlockSpec(memory_space=vmem)] * 3,
        out_specs=(pl.BlockSpec(memory_space=vmem),) * 2,
        compiler_params=pltpu.CompilerParams(vmem_limit_bytes=60 * 1024 * 1024),
        name="settle",
    )(
        moved_from.reshape(1, -1),
        landed_level.reshape(n * slots, cells),
        landed_flow.reshape(n * slots, wide),
    )
    return level, flow.reshape(blocks, 2, cells)


def solution(mesh):
    n = mesh.shape["dom"]
    return jax.shard_map(
        functools.partial(local, n),
        mesh=mesh,
        in_specs=(
            P("dom", None),
            P("dom", None, None),
            P("dom", None),
            P("dom", None),
            P(),
            P(),
            P("dom", None),
            P(None, "dom"),
            P("dom"),
            P("dom"),
            P(None, "dom"),
            P("dom"),
        ),
        out_specs=(P("dom", None), P("dom", None, None)),
        check_vma=False,
    )
```

```python
import functools

import jax
import jax.numpy as jnp
from jax import lax
from jax.experimental import pallas as pl
from jax.experimental.pallas import tpu as pltpu
from jax.sharding import PartitionSpec as P

MESH = pl.DeviceIdType.MESH
f32 = jnp.float32
bf16 = jnp.bfloat16
relax_rate = 0.5


def halves(x):
    hi = x.astype(bf16)
    return hi, (x - hi.astype(f32)).astype(bf16)


def mm(a, b):
    return jnp.dot(a, b, preferred_element_type=f32)


def mm3(hi, lo, w_hi, w_lo):
    return mm(hi, w_hi) + (mm(lo, w_hi) + mm(hi, w_lo))


def hot(cond):
    return jnp.where(cond, 1.0, 0.0).astype(f32)


def iota(shape, dim):
    return lax.broadcasted_iota(jnp.int32, shape, dim).astype(f32)


def kernel(
    n, slots,
    elev_hbm, mom_hbm, depth_hbm, drag_hbm, divw_hbm, gradw_hbm, nb_hbm, wet_hbm,
    cells_hbm, source_hbm, series_hbm, moved_hbm,
    landed_level, landed_flow,
    elev_ref, mom_ref, depth_ref, drag_ref, divw_ref, gradw_ref, nb_ref, wet_ref,
    cells_ref, source_ref, series_ref, moved_ref,
    meta, gathered, x_ref, dl_hi, dl_lo, ds_hi, ds_lo, gl_hi, gl_lo, gs_hi, gs_lo,
    damp_ref, depth_p, near_rows, near_cols, div_ref, grad_ref,
    force_ref, relax_ref, div_send, div_recv, lev_send, lev_recv, pack, packed_level, packed_flow,
    in_ss, meta_ss, meta_rs, div_ss, div_rs, lev_ss, lev_rs, mig_ss, mig_rs, own_ss,
):
    me = lax.axis_index("dom")
    steps, width = series_ref.shape
    blocks, cells = elev_ref.shape
    half = blocks // 2
    wide = 2 * cells
    span = blocks // width

    inputs = [
        pltpu.make_async_copy(src, dst, in_ss.at[i])
        for i, (src, dst) in enumerate(
            (
                (nb_hbm, nb_ref),
                (moved_hbm, moved_ref),
                (series_hbm, series_ref),
                (wet_hbm, wet_ref),
                (cells_hbm, cells_ref),
                (source_hbm, source_ref),
                (mom_hbm, mom_ref),
                (elev_hbm, elev_ref),
                (depth_hbm, depth_ref),
                (drag_hbm, drag_ref),
                (divw_hbm, divw_ref),
                (gradw_hbm, gradw_ref),
            )
        )
    ]
    for copy in inputs:
        copy.start()

    barrier = pltpu.get_barrier_semaphore()

    def greet(i, _):
        pl.semaphore_signal(
            barrier, inc=1, device_id=(lax.rem(me + i, n),), device_id_type=MESH
        )
        return 0

    lax.fori_loop(1, n, greet, 0)

    def partner(i):
        j = i - 1
        return lax.rem(me + (j + 1) // 2 + (1 - j % 2) * (n // 2), n)

    def sl(k, size):
        return slice(k * size, (k + 1) * size)

    near_half, far_half = 1 - lax.rem(me, 2), lax.rem(me, 2)

    def rows_of(h):
        return pl.ds(pl.multiple_of(h * half, half), half)

    for copy in inputs[:6]:
        copy.wait()
    base = (me * blocks).astype(f32)
    square = (blocks, blocks)
    sub, lane = iota(square, 0), iota(square, 1)
    nb = nb_ref[...].astype(f32)
    nbl = nb - base
    lower_own = jnp.logical_and(nbl[2:3] >= 0.0, nbl[2:3] < float(blocks))
    key_row = jnp.where(lower_own, nb[3:4] + float(blocks), lane[0:1])
    key_col = jnp.sum(jnp.where(sub == lane, key_row, 0.0), axis=1, keepdims=True)
    pos_row = jnp.sum(hot(key_col < key_row), axis=0, keepdims=True)
    pos_col = jnp.sum(hot(key_row < key_col), axis=1, keepdims=True)
    order = hot(sub == pos_row)
    order16 = order.astype(bf16)

    for copy in inputs[6:10]:
        copy.wait()
    field = jnp.concatenate(
        [
            mom_ref[pl.ds(0, blocks, 2), :],
            mom_ref[pl.ds(1, blocks, 2), :],
            elev_ref[...],
            depth_ref[...],
            drag_ref[...],
        ],
        axis=1,
    )
    hi, lo = halves(field)
    field = mm(order16, hi) + mm(order16, lo)
    x_ref[...] = field[:, :wide]
    elevation0 = field[:, wide : 3 * cells]
    depth_p[...] = field[:, 3 * cells : 4 * cells]
    damping = 1.0 / (1.0 + field[:, 4 * cells :])
    inputs[10].wait()
    for half_w, local_w, send_w in zip(halves(divw_ref[...]), (dl_hi, dl_lo), (ds_hi, ds_lo)):
        slot = [half_w[sl(k, wide), :] for k in range(5)]
        local_w[0] = jnp.concatenate([slot[0], slot[1]], axis=1)
        for h in (0, 1):
            local_w[1 + h] = jnp.concatenate([slot[2], slot[3 + h]], axis=1)
            send_w[h] = slot[4 - h]

    def halo(send, recv, ss, rs, step, h):
        return pltpu.make_async_remote_copy(
            src_ref=send,
            dst_ref=recv.at[step, 1 - h],
            send_sem=ss.at[step, h],
            recv_sem=rs.at[step, 1 - h],
            device_id=(lax.rem(me + 2 * h - 1 + n, n),),
            device_id_type=MESH,
        )

    def div_copy(step, h):
        return halo(div_send.at[step, h], div_recv, div_ss, div_rs, step, h)

    def lev_copy(step, h):
        return halo(lev_send.at[step + 1, rows_of(h)], lev_recv, lev_ss, lev_rs, step, h)

    def shed(step, h):
        hi, lo = halves(x_ref[rows_of(h), :])
        div_send[step, h] = mm3(hi, lo, ds_hi[h], ds_lo[h])

    def tile_copy(target, source):
        return pltpu.make_async_remote_copy(
            src_ref=meta,
            dst_ref=gathered.at[source],
            send_sem=meta_ss,
            recv_sem=meta_rs,
            device_id=(target,),
            device_id_type=MESH,
        )

    def state_copy(kind, target, source):
        src, dst = ((packed_level, landed_level), (packed_flow, landed_flow))[kind]
        return pltpu.make_async_remote_copy(
            src_ref=src.at[target],
            dst_ref=dst.at[source],
            send_sem=mig_ss.at[kind],
            recv_sem=mig_rs.at[kind],
            device_id=(target,),
            device_id_type=MESH,
        )

    def all_done(ref, sem):
        others = ref.at[pl.ds(0, n - 1)]
        pltpu.make_async_copy(others, others, sem).wait()

    def own_copy(kind):
        src, dst = ((packed_level, landed_level), (packed_flow, landed_flow))[kind]
        return pltpu.make_async_copy(src.at[me], dst.at[me], own_ss.at[kind])

    def migrate(kind, hi, lo):
        src = (packed_level, packed_flow)[kind]
        src[...] = (mm(pack[...], hi) + mm(pack[...], lo)).reshape(src.shape)

        def send(i, _):
            state_copy(kind, partner(i), me).start()
            return 0

        lax.fori_loop(1, n, send, 0)
        own_copy(kind).start()

    moved = moved_ref[...].astype(f32)

    def open_up():
        meta[...] = jnp.zeros_like(meta)
        meta[0:steps, :] = series_ref[...]
        for i in range(span):
            meta[steps + i : steps + i + 1, :] = moved[:, i * width : (i + 1) * width]
        gathered[pl.ds(me, 1)] = meta[...][None]
        pl.semaphore_wait(barrier, n - 1)

    def send_tiles():
        def send(i, _):
            tile_copy(partner(i), me).start()
            return 0

        lax.fori_loop(1, n, send, 0)

        def place(ids):
            return jnp.sum(jnp.where(sub == ids, pos_col, 0.0), axis=0, keepdims=True)

        vertical = jnp.where(lower_own, nbl[2:3], nbl[3:4])
        for k, ids in enumerate((nbl[0:1], nbl[1:2], vertical)):
            col = jnp.sum(order * place(ids), axis=1, keepdims=True)
            near = hot(lane == col).astype(bf16)
            near_rows[sl(k, blocks), :] = near
            near_cols[:, sl(k, blocks)] = near
        wet = wet_ref[...].astype(f32)
        for s in range(steps):
            mask = jnp.sum(order * wet[s : s + 1], axis=1, keepdims=True)
            damp_ref[s, :, :cells] = jnp.broadcast_to(mask, (blocks, cells))
            damp_ref[s, :, cells:] = mask * damping

    def boundary():
        entries = cells_ref.shape[1]
        point = source_ref[...].astype(f32)
        chunk = jnp.floor((point + 0.5) * (1.0 / width))
        spot = point - chunk * width
        pick = hot(iota((width, entries), 0) == spot).astype(bf16)
        cell = cells_ref[...].astype(f32)
        block = jnp.floor((cell + 0.5) * (1.0 / cells))
        element = cell - block * cells
        block_place = jnp.sum(
            jnp.where(iota((blocks, entries), 0) == block, pos_col, 0.0), axis=0, keepdims=True
        )
        rows = hot(iota((blocks, entries), 0) == block_place).astype(bf16)
        columns = hot(iota((cells, entries), 0) == element)

        def spread(values):
            return lax.dot_general(
                rows, values, (((1,), (1,)), ((), ())), preferred_element_type=f32
            )

        relax_ref[...] = relax_rate * spread(columns.astype(bf16))

        all_done(gathered, meta_rs)
        tall = meta.shape[0]
        hi, lo = halves(gathered[...].reshape(n * tall, width))
        found = (mm(hi, pick) + mm(lo, pick)).reshape(n, tall, entries)
        found = jnp.sum(jnp.where(iota(found.shape, 0) == chunk[None], found, 0.0), axis=0)
        for s in range(steps):
            hi, lo = halves(columns * found[s : s + 1])
            force_ref[s] = spread(hi) + spread(lo)

    def choose():
        everyone = gathered[...]
        takes = jnp.concatenate([everyone[:, steps + i, :] for i in range(span)], axis=1) - base
        mine = hot(jnp.logical_and(takes >= 0.0, takes < float(blocks)))
        rank = mm(mine.astype(bf16), hot(sub < lane).astype(bf16))
        rank = jnp.where(mine > 0.0, rank, -1.0)
        cube = (n, slots, blocks)
        chosen = jnp.where(rank[:, None, :] == iota(cube, 1), takes[:, None, :] + 1.0, 0.0)
        chosen = jnp.sum(chosen.reshape(n * slots, blocks), axis=1, keepdims=True) - 1.0
        lanes = iota((n * slots, blocks), 1)
        pack[...] = mm(
            hot(lanes == chosen).astype(bf16), hot(lane == pos_col).astype(bf16)
        ).astype(bf16)

    def one_step(step, opening, closing):
        if opening:
            open_up()
            for h in (far_half, near_half):
                div_copy(step, h).start()
            send_tiles()
        hi, lo = halves(x_ref[...])
        first = mm3(hi, lo, dl_hi[0], dl_lo[0])
        second = jnp.concatenate(
            [
                mm3(hi[sl(h, half)], lo[sl(h, half)], dl_hi[1 + h], dl_lo[1 + h])
                for h in (0, 1)
            ],
            axis=0,
        )
        parts = jnp.concatenate([first[:, cells:], second[:, :cells], second[:, cells:]], axis=0)
        parts = mm(near_cols[...], jnp.concatenate(halves(parts), axis=1))
        div_ref[...] = first[:, :cells] + (parts[:, :cells] + parts[:, cells:])
        if opening:
            boundary()
        for h in (near_half, far_half):
            r = rows_of(h)
            div_copy(step, 1 - h).wait_recv()
            div = div_ref[r, :] + div_recv[step, h]
            level = lev_send[step, r, :] - damp_ref[step, r, :cells] * div
            lev_send[step + 1, r, :] = level + relax_ref[r, :] * (force_ref[step, r, :] - level)
            lev_copy(step, h).start()
        if opening:
            inputs[11].wait()
            for half_w, local_w, away_w in zip(
                halves(gradw_ref[...]), (gl_hi, gl_lo), (gs_hi, gs_lo)
            ):
                slot = [half_w[sl(k, cells), :] for k in range(5)]
                for h in (0, 1):
                    local_w[h] = jnp.concatenate(slot[:3] + [slot[4 - h]], axis=0)
                    away_w[h] = slot[3 + h]
        hi, lo = halves(lev_send[step + 1])
        near = mm(near_rows[...], jnp.concatenate([hi, lo], axis=1)).astype(bf16)
        near = [near[sl(k, blocks)] for k in range(3)]
        hi4 = jnp.concatenate([hi] + [p[:, :cells] for p in near], axis=1)
        lo4 = jnp.concatenate([lo] + [p[:, cells:] for p in near], axis=1)
        for h in (0, 1):
            r = sl(h, half)
            grad_ref[r, :] = mm3(hi4[r], lo4[r], gl_hi[h], gl_lo[h])
        if opening:
            choose()
        if closing:
            migrate(0, hi, lo)
        for h in (near_half, far_half):
            r = rows_of(h)
            lev_copy(step, 1 - h).wait_recv()
            grad = grad_ref[r, :] + mm3(*halves(lev_recv[step, h]), gs_hi[h], gs_lo[h])
            depth = depth_p[r, :]
            damp = damp_ref[step, r, cells:]
            x_ref[r, :cells] = damp * (x_ref[r, :cells] - depth * grad[:, :cells])
            x_ref[r, cells:] = damp * (x_ref[r, cells:] - depth * grad[:, cells:])
            if not closing:
                shed(step + 1, h)
                div_copy(step + 1, h).start()

    lev_send[0] = elevation0
    for h in (0, 1):
        shed(0, h)
    one_step(0, True, False)

    def middle(step, _):
        one_step(step, False, False)
        return 0

    lax.fori_loop(1, steps - 1, middle, 0)
    one_step(steps - 1, False, True)
    migrate(1, *halves(x_ref[...]))

    def halo_sent(step, _):
        for h in (0, 1):
            div_copy(step, h).wait_send()
            lev_copy(step, h).wait_send()
        return 0

    lax.fori_loop(0, steps, halo_sent, 0)
    all_done(gathered, meta_ss)
    for kind, src, dst in ((0, packed_level, landed_level), (1, packed_flow, landed_flow)):
        own_copy(kind).wait()
        all_done(src, mig_ss.at[kind])
        all_done(dst, mig_rs.at[kind])


def settle(slots, moved_ref, landed_level, landed_flow, level_out, flow_out):
    blocks, cells = level_out.shape
    places = landed_level.shape[0]
    square = (blocks, blocks)
    sub, lane = iota(square, 0), iota(square, 1)
    owner_row = jnp.floor((moved_ref[...].astype(f32) + 0.5) * (1.0 / blocks))
    owner_col = jnp.sum(jnp.where(sub == lane, owner_row, 0.0), axis=1, keepdims=True)
    ahead = jnp.sum(
        jnp.where(lane < sub, hot(owner_row == owner_col), 0.0), axis=1, keepdims=True
    )
    where_from = owner_col * float(slots) + ahead
    unpack = hot(iota((blocks, places), 1) == where_from).astype(bf16)
    hi, lo = halves(landed_level[...])
    level_out[...] = mm(unpack, hi) + mm(unpack, lo)
    hi, lo = halves(landed_flow[...])
    flow = mm(unpack, hi) + mm(unpack, lo)
    flow_out[pl.ds(0, blocks, 2), :] = flow[:, :cells]
    flow_out[pl.ds(1, blocks, 2), :] = flow[:, cells:]


def local(
    n,
    elevation,
    momentum,
    depth,
    drag,
    div_weight,
    grad_weight,
    neighbours,
    wet,
    boundary_cells,
    boundary_source,
    series,
    moved_from,
):
    blocks, cells = elevation.shape
    steps, width = series.shape
    half = blocks // 2
    wide = 2 * cells
    portion = 2 * blocks // n
    slots = -(-portion // 8) * 8
    tall = -(-(steps + blocks // width) // 8) * 8
    vmem, dma = pltpu.VMEM, pltpu.SemaphoreType.DMA
    landed_level, landed_flow = pl.pallas_call(
        functools.partial(kernel, n, slots),
        out_shape=(
            jax.ShapeDtypeStruct((n, slots, cells), f32),
            jax.ShapeDtypeStruct((n, slots, wide), f32),
        ),
        in_specs=[pl.BlockSpec(memory_space=pl.ANY)] * 12,
        out_specs=(pl.BlockSpec(memory_space=pl.ANY),) * 2,
        scratch_shapes=[
            vmem((blocks, cells), f32),
            vmem((2 * blocks, cells), f32),
            vmem((blocks, cells), f32),
            vmem((blocks, cells), f32),
            vmem((5 * wide, cells), f32),
            vmem((5 * cells, wide), f32),
            vmem((4, blocks), jnp.int32),
            vmem(wet.shape, jnp.int32),
            vmem((1, boundary_cells.shape[0]), jnp.int32),
            vmem((1, boundary_source.shape[0]), jnp.int32),
            vmem(series.shape, f32),
            vmem((1, blocks), jnp.int32),
            vmem((tall, width), f32),
            vmem((n, tall, width), f32),
            vmem((blocks, wide), f32),
            vmem((3, wide, wide), bf16),
            vmem((3, wide, wide), bf16),
            vmem((2, wide, cells), bf16),
            vmem((2, wide, cells), bf16),
            vmem((2, 4 * cells, wide), bf16),
            vmem((2, 4 * cells, wide), bf16),
            vmem((2, cells, wide), bf16),
            vmem((2, cells, wide), bf16),
            vmem((steps, blocks, wide), f32),
            vmem((blocks, cells), f32),
            vmem((3 * blocks, blocks), bf16),
            vmem((blocks, 3 * blocks), bf16),
            vmem((blocks, cells), f32),
            vmem((blocks, wide), f32),
            vmem((steps, blocks, cells), f32),
            vmem((blocks, cells), f32),
            vmem((steps, 2, half, cells), f32),
            vmem((steps, 2, half, cells), f32),
            vmem((steps + 1, blocks, cells), f32),
            vmem((steps, 2, half, cells), f32),
            vmem((n * slots, blocks), bf16),
            vmem((n, slots, cells), f32),
            vmem((n, slots, wide), f32),
            dma((12,)),
            dma,
            dma,
            dma((steps, 2)),
            dma((steps, 2)),
            dma((steps, 2)),
            dma((steps, 2)),
            dma((2,)),
            dma((2,)),
            dma((2,)),
        ],
        compiler_params=pltpu.CompilerParams(
            collective_id=0, has_side_effects=True, vmem_limit_bytes=60 * 1024 * 1024
        ),
        name="surge",
    )(
        elevation,
        momentum.reshape(2 * blocks, cells),
        depth,
        drag,
        div_weight.reshape(5 * wide, cells),
        grad_weight.reshape(5 * cells, wide),
        neighbours.T,
        wet,
        boundary_cells.reshape(1, -1),
        boundary_source.reshape(1, -1),
        series,
        moved_from.reshape(1, -1),
    )
    level, flow = pl.pallas_call(
        functools.partial(settle, slots),
        out_shape=(
            jax.ShapeDtypeStruct((blocks, cells), f32),
            jax.ShapeDtypeStruct((2 * blocks, cells), f32),
        ),
        in_specs=[pl.BlockSpec(memory_space=vmem)] * 3,
        out_specs=(pl.BlockSpec(memory_space=vmem),) * 2,
        compiler_params=pltpu.CompilerParams(vmem_limit_bytes=60 * 1024 * 1024),
        name="settle",
    )(
        moved_from.reshape(1, -1),
        landed_level.reshape(n * slots, cells),
        landed_flow.reshape(n * slots, wide),
    )
    return level, flow.reshape(blocks, 2, cells)


def solution(mesh):
    n = mesh.shape["dom"]
    return jax.shard_map(
        functools.partial(local, n),
        mesh=mesh,
        in_specs=(
            P("dom", None),
            P("dom", None, None),
            P("dom", None),
            P("dom", None),
            P(),
            P(),
            P("dom", None),
            P(None, "dom"),
            P("dom"),
            P("dom"),
            P(None, "dom"),
            P("dom"),
        ),
        out_specs=(P("dom", None), P("dom", None, None)),
        check_vma=False,
    )
```

```python
import functools

import jax
import jax.numpy as jnp
from jax import lax
from jax.experimental import pallas as pl
from jax.experimental.pallas import tpu as pltpu
from jax.sharding import PartitionSpec as P

MESH = pl.DeviceIdType.MESH
f32 = jnp.float32
bf16 = jnp.bfloat16
relax_rate = 0.5


def halves(x):
    hi = x.astype(bf16)
    return hi, (x - hi.astype(f32)).astype(bf16)


def mm(a, b):
    return jnp.dot(a, b, preferred_element_type=f32)


def mm3(hi, lo, w_hi, w_lo):
    return mm(hi, w_hi) + (mm(lo, w_hi) + mm(hi, w_lo))


def hot(cond):
    return jnp.where(cond, 1.0, 0.0).astype(f32)


def iota(shape, dim):
    return lax.broadcasted_iota(jnp.int32, shape, dim).astype(f32)


def kernel(
    n, slots,
    elev_hbm, mom_hbm, depth_hbm, drag_hbm, divw_hbm, gradw_hbm, nb_hbm, wet_hbm,
    cells_hbm, source_hbm, series_hbm, moved_hbm,
    landed_level, landed_flow,
    elev_ref, mom_ref, depth_ref, drag_ref, divw_ref, gradw_ref, nb_ref, wet_ref,
    cells_ref, source_ref, series_ref, moved_ref,
    meta, gathered, x_ref, dl_hi, dl_lo, ds_both, gl_hi, gl_lo, gs_twice, gs_lo,
    damp_ref, depth_p, near_rows, near_cols, div_ref, grad_ref,
    force_ref, relax_ref, div_send, div_recv, lev_send, lev_recv, pack, packed_level, packed_flow,
    in_ss, meta_ss, meta_rs, div_ss, div_rs, lev_ss, lev_rs, mig_ss, mig_rs, own_ss,
):
    me = lax.axis_index("dom")
    steps, width = series_ref.shape
    blocks, cells = elev_ref.shape
    half = blocks // 2
    wide = 2 * cells
    span = blocks // width

    inputs = [
        pltpu.make_async_copy(src, dst, in_ss.at[i])
        for i, (src, dst) in enumerate(
            (
                (nb_hbm, nb_ref),
                (moved_hbm, moved_ref),
                (series_hbm, series_ref),
                (wet_hbm, wet_ref),
                (cells_hbm, cells_ref),
                (source_hbm, source_ref),
                (mom_hbm, mom_ref),
                (elev_hbm, elev_ref),
                (depth_hbm, depth_ref),
                (drag_hbm, drag_ref),
                (divw_hbm, divw_ref),
                (gradw_hbm, gradw_ref),
            )
        )
    ]
    for copy in inputs:
        copy.start()

    barrier = pltpu.get_barrier_semaphore()

    def greet(i, _):
        pl.semaphore_signal(
            barrier, inc=1, device_id=(lax.rem(me + i, n),), device_id_type=MESH
        )
        return 0

    lax.fori_loop(1, n, greet, 0)

    def partner(i):
        j = i - 1
        return lax.rem(me + (j + 1) // 2 + (1 - j % 2) * (n // 2), n)

    def sl(k, size):
        return slice(k * size, (k + 1) * size)

    near_half, far_half = 1 - lax.rem(me, 2), lax.rem(me, 2)

    near_pieces = [(near_half, 0, 0, half)]
    far_pieces = [(far_half, i, i * (half // 2), half // 2) for i in (0, 1)]

    def rows_of(piece):
        h, _, first, size = piece
        return pl.ds(pl.multiple_of(h * half + first, half // 2), size)

    for copy in inputs[:6]:
        copy.wait()
    base = (me * blocks).astype(f32)
    square = (blocks, blocks)
    sub, lane = iota(square, 0), iota(square, 1)
    nb = nb_ref[...].astype(f32)
    nbl = nb - base
    lower_own = jnp.logical_and(nbl[2:3] >= 0.0, nbl[2:3] < float(blocks))
    key_row = jnp.where(lower_own, nb[3:4] + float(blocks), lane[0:1])
    key_col = jnp.sum(jnp.where(sub == lane, key_row, 0.0), axis=1, keepdims=True)
    pos_row = jnp.sum(hot(key_col < key_row), axis=0, keepdims=True)
    pos_col = jnp.sum(hot(key_row < key_col), axis=1, keepdims=True)
    order = hot(sub == pos_row)
    order16 = order.astype(bf16)

    for copy in inputs[6:10]:
        copy.wait()
    field = jnp.concatenate(
        [
            mom_ref[pl.ds(0, blocks, 2), :],
            mom_ref[pl.ds(1, blocks, 2), :],
            elev_ref[...],
            depth_ref[...],
            drag_ref[...],
        ],
        axis=1,
    )
    hi, lo = halves(field)
    field = mm(order16, hi) + mm(order16, lo)
    x_ref[...] = field[:, :wide]
    elevation0 = field[:, wide : 3 * cells]
    depth_p[...] = field[:, 3 * cells : 4 * cells]
    damping = 1.0 / (1.0 + field[:, 4 * cells :])
    inputs[10].wait()
    hi, lo = halves(divw_ref[...])
    for half_w, local_w in ((hi, dl_hi), (lo, dl_lo)):
        slot = [half_w[sl(k, wide), :] for k in range(5)]
        local_w[0] = jnp.concatenate([slot[0], slot[1]], axis=1)
        for h in (0, 1):
            local_w[1 + h] = jnp.concatenate([slot[2], slot[3 + h]], axis=1)
    for h in (0, 1):
        ds_both[h] = jnp.concatenate([hi[sl(4 - h, wide), :], lo[sl(4 - h, wide), :]], axis=1)

    def halo(src, recv, ss, rs, step, piece):
        h, i, first, size = piece
        return pltpu.make_async_remote_copy(
            src_ref=src,
            dst_ref=recv.at[step, 1 - h, pl.ds(first, size)],
            send_sem=ss.at[step, h, i],
            recv_sem=rs.at[step, 1 - h, i],
            device_id=(lax.rem(me + 2 * h - 1 + n, n),),
            device_id_type=MESH,
        )

    def div_copy(step, piece):
        h, _, first, size = piece
        src = div_send.at[step, h, pl.ds(first, size)]
        return halo(src, div_recv, div_ss, div_rs, step, piece)

    def lev_copy(step, piece):
        src = lev_send.at[step + 1, rows_of(piece)]
        return halo(src, lev_recv, lev_ss, lev_rs, step, piece)

    def facing(piece):
        return (1 - piece[0],) + piece[1:]

    def shed(step, piece):
        h, _, first, size = piece
        hi, lo = halves(x_ref[rows_of(piece), :])
        both = mm(hi, ds_both[h])
        rest = mm(lo, ds_both[h, :, :cells])
        div_send[step, h, first : first + size] = both[:, :cells] + (both[:, cells:] + rest)

    def tile_copy(target, source):
        return pltpu.make_async_remote_copy(
            src_ref=meta,
            dst_ref=gathered.at[source],
            send_sem=meta_ss,
            recv_sem=meta_rs,
            device_id=(target,),
            device_id_type=MESH,
        )

    def state_copy(kind, target, source):
        src, dst = ((packed_level, landed_level), (packed_flow, landed_flow))[kind]
        return pltpu.make_async_remote_copy(
            src_ref=src.at[target],
            dst_ref=dst.at[source],
            send_sem=mig_ss.at[kind],
            recv_sem=mig_rs.at[kind],
            device_id=(target,),
            device_id_type=MESH,
        )

    def all_done(ref, sem):
        others = ref.at[pl.ds(0, n - 1)]
        pltpu.make_async_copy(others, others, sem).wait()

    def own_copy(kind):
        src, dst = ((packed_level, landed_level), (packed_flow, landed_flow))[kind]
        return pltpu.make_async_copy(src.at[me], dst.at[me], own_ss.at[kind])

    def migrate(kind, hi, lo):
        src = (packed_level, packed_flow)[kind]
        src[...] = (mm(pack[...], hi) + mm(pack[...], lo)).reshape(src.shape)

        def send(i, _):
            state_copy(kind, partner(i), me).start()
            return 0

        lax.fori_loop(1, n, send, 0)
        own_copy(kind).start()

    moved = moved_ref[...].astype(f32)

    def open_up():
        meta[...] = jnp.zeros_like(meta)
        meta[0:steps, :] = series_ref[...]
        for i in range(span):
            meta[steps + i : steps + i + 1, :] = moved[:, i * width : (i + 1) * width]
        gathered[pl.ds(me, 1)] = meta[...][None]
        pl.semaphore_wait(barrier, n - 1)

    def send_tiles():
        def send(i, _):
            tile_copy(partner(i), me).start()
            return 0

        lax.fori_loop(1, n, send, 0)

        def place(ids):
            return jnp.sum(jnp.where(sub == ids, pos_col, 0.0), axis=0, keepdims=True)

        vertical = jnp.where(lower_own, nbl[2:3], nbl[3:4])
        for k, ids in enumerate((nbl[0:1], nbl[1:2], vertical)):
            col = jnp.sum(order * place(ids), axis=1, keepdims=True)
            near = hot(lane == col).astype(bf16)
            near_rows[sl(k, blocks), :] = near
            near_cols[:, sl(k, blocks)] = near
        wet = wet_ref[...].astype(f32)
        for s in range(steps):
            mask = jnp.sum(order * wet[s : s + 1], axis=1, keepdims=True)
            damp_ref[s, :, :cells] = jnp.broadcast_to(mask, (blocks, cells))
            damp_ref[s, :, cells:] = mask * damping

    def boundary():
        entries = cells_ref.shape[1]
        point = source_ref[...].astype(f32)
        chunk = jnp.floor((point + 0.5) * (1.0 / width))
        spot = point - chunk * width
        pick = hot(iota((width, entries), 0) == spot).astype(bf16)
        cell = cells_ref[...].astype(f32)
        block = jnp.floor((cell + 0.5) * (1.0 / cells))
        element = cell - block * cells
        block_place = jnp.sum(
            jnp.where(iota((blocks, entries), 0) == block, pos_col, 0.0), axis=0, keepdims=True
        )
        rows = hot(iota((blocks, entries), 0) == block_place).astype(bf16)
        columns = hot(iota((cells, entries), 0) == element)

        def spread(values):
            return lax.dot_general(
                rows, values, (((1,), (1,)), ((), ())), preferred_element_type=f32
            )

        relax_ref[...] = relax_rate * spread(columns.astype(bf16))

        all_done(gathered, meta_rs)
        tall = meta.shape[0]
        hi, lo = halves(gathered[...].reshape(n * tall, width))
        found = (mm(hi, pick) + mm(lo, pick)).reshape(n, tall, entries)
        found = jnp.sum(jnp.where(iota(found.shape, 0) == chunk[None], found, 0.0), axis=0)
        for s in range(steps):
            hi, lo = halves(columns * found[s : s + 1])
            force_ref[s] = spread(hi) + spread(lo)

    def choose():
        everyone = gathered[...]
        takes = jnp.concatenate([everyone[:, steps + i, :] for i in range(span)], axis=1) - base
        mine = hot(jnp.logical_and(takes >= 0.0, takes < float(blocks)))
        rank = mm(mine.astype(bf16), hot(sub < lane).astype(bf16))
        rank = jnp.where(mine > 0.0, rank, -1.0)
        cube = (n, slots, blocks)
        chosen = jnp.where(rank[:, None, :] == iota(cube, 1), takes[:, None, :] + 1.0, 0.0)
        chosen = jnp.sum(chosen.reshape(n * slots, blocks), axis=1, keepdims=True) - 1.0
        lanes = iota((n * slots, blocks), 1)
        pack[...] = mm(
            hot(lanes == chosen).astype(bf16), hot(lane == pos_col).astype(bf16)
        ).astype(bf16)

    def one_step(step, opening, closing):
        if opening:
            open_up()
            for piece in far_pieces + near_pieces:
                div_copy(step, piece).start()
            send_tiles()
        hi, lo = halves(x_ref[...])
        first = mm3(hi, lo, dl_hi[0], dl_lo[0])
        second = jnp.concatenate(
            [
                mm3(hi[sl(h, half)], lo[sl(h, half)], dl_hi[1 + h], dl_lo[1 + h])
                for h in (0, 1)
            ],
            axis=0,
        )
        parts = jnp.concatenate([first[:, cells:], second[:, :cells], second[:, cells:]], axis=0)
        parts = mm(near_cols[...], jnp.concatenate(halves(parts), axis=1))
        div_ref[...] = first[:, :cells] + (parts[:, :cells] + parts[:, cells:])
        if opening:
            boundary()
        for piece in near_pieces + far_pieces:
            h, _, first, size = piece
            r = rows_of(piece)
            div_copy(step, facing(piece)).wait_recv()
            div = div_ref[r, :] + div_recv[step, h, first : first + size]
            level = lev_send[step, r, :] - damp_ref[step, r, :cells] * div
            lev_send[step + 1, r, :] = level + relax_ref[r, :] * (force_ref[step, r, :] - level)
            lev_copy(step, piece).start()
        if opening:
            inputs[11].wait()
            hi, lo = halves(gradw_ref[...])
            for half_w, local_w in ((hi, gl_hi), (lo, gl_lo)):
                slot = [half_w[sl(k, cells), :] for k in range(5)]
                for h in (0, 1):
                    local_w[h] = jnp.concatenate(slot[:3] + [slot[4 - h]], axis=0)
            for h in (0, 1):
                gs_twice[h] = jnp.concatenate([hi[sl(3 + h, cells), :]] * 2, axis=0)
                gs_lo[h] = lo[sl(3 + h, cells), :]
        hi, lo = halves(lev_send[step + 1])
        if closing:
            migrate(0, hi, lo)
        near = mm(near_rows[...], jnp.concatenate([hi, lo], axis=1)).astype(bf16)
        near = [near[sl(k, blocks)] for k in range(3)]
        hi4 = jnp.concatenate([hi] + [p[:, :cells] for p in near], axis=1)
        lo4 = jnp.concatenate([lo] + [p[:, cells:] for p in near], axis=1)
        for h in (0, 1):
            r = sl(h, half)
            grad_ref[r, :] = mm3(hi4[r], lo4[r], gl_hi[h], gl_lo[h])
        if opening:
            choose()
        for piece in near_pieces + far_pieces:
            h, _, first, size = piece
            r = rows_of(piece)
            lev_copy(step, facing(piece)).wait_recv()
            hi, lo = halves(lev_recv[step, h, first : first + size])
            grad = mm(jnp.concatenate([hi, lo], axis=1), gs_twice[h]) + mm(hi, gs_lo[h])
            grad = grad_ref[r, :] + grad
            depth = depth_p[r, :]
            damp = damp_ref[step, r, cells:]
            x_ref[r, :cells] = damp * (x_ref[r, :cells] - depth * grad[:, :cells])
            x_ref[r, cells:] = damp * (x_ref[r, cells:] - depth * grad[:, cells:])
            if not closing:
                shed(step + 1, piece)
                div_copy(step + 1, piece).start()

    lev_send[0] = elevation0
    for piece in far_pieces + near_pieces:
        shed(0, piece)
    one_step(0, True, False)

    def middle(step, _):
        one_step(step, False, False)
        return 0

    lax.fori_loop(1, steps - 1, middle, 0)
    one_step(steps - 1, False, True)
    migrate(1, *halves(x_ref[...]))

    def halo_sent(step, _):
        for piece in near_pieces + far_pieces:
            div_copy(step, piece).wait_send()
            lev_copy(step, piece).wait_send()
        return 0

    lax.fori_loop(0, steps, halo_sent, 0)
    all_done(gathered, meta_ss)
    for kind, src, dst in ((0, packed_level, landed_level), (1, packed_flow, landed_flow)):
        own_copy(kind).wait()
        all_done(src, mig_ss.at[kind])
        all_done(dst, mig_rs.at[kind])


def settle(slots, moved_ref, landed_level, landed_flow, level_out, flow_out):
    blocks, cells = level_out.shape
    places = landed_level.shape[0]
    square = (blocks, blocks)
    sub, lane = iota(square, 0), iota(square, 1)
    owner_row = jnp.floor((moved_ref[...].astype(f32) + 0.5) * (1.0 / blocks))
    owner_col = jnp.sum(jnp.where(sub == lane, owner_row, 0.0), axis=1, keepdims=True)
    ahead = jnp.sum(
        jnp.where(lane < sub, hot(owner_row == owner_col), 0.0), axis=1, keepdims=True
    )
    where_from = owner_col * float(slots) + ahead
    unpack = hot(iota((blocks, places), 1) == where_from).astype(bf16)
    hi, lo = halves(landed_level[...])
    level_out[...] = mm(unpack, hi) + mm(unpack, lo)
    hi, lo = halves(landed_flow[...])
    flow = mm(unpack, hi) + mm(unpack, lo)
    flow_out[pl.ds(0, blocks, 2), :] = flow[:, :cells]
    flow_out[pl.ds(1, blocks, 2), :] = flow[:, cells:]


def local(
    n,
    elevation,
    momentum,
    depth,
    drag,
    div_weight,
    grad_weight,
    neighbours,
    wet,
    boundary_cells,
    boundary_source,
    series,
    moved_from,
):
    blocks, cells = elevation.shape
    steps, width = series.shape
    half = blocks // 2
    wide = 2 * cells
    portion = 2 * blocks // n
    slots = -(-portion // 8) * 8
    tall = -(-(steps + blocks // width) // 8) * 8
    vmem, dma = pltpu.VMEM, pltpu.SemaphoreType.DMA
    landed_level, landed_flow = pl.pallas_call(
        functools.partial(kernel, n, slots),
        out_shape=(
            jax.ShapeDtypeStruct((n, slots, cells), f32),
            jax.ShapeDtypeStruct((n, slots, wide), f32),
        ),
        in_specs=[pl.BlockSpec(memory_space=pl.ANY)] * 12,
        out_specs=(pl.BlockSpec(memory_space=pl.ANY),) * 2,
        scratch_shapes=[
            vmem((blocks, cells), f32),
            vmem((2 * blocks, cells), f32),
            vmem((blocks, cells), f32),
            vmem((blocks, cells), f32),
            vmem((5 * wide, cells), f32),
            vmem((5 * cells, wide), f32),
            vmem((4, blocks), jnp.int32),
            vmem(wet.shape, jnp.int32),
            vmem((1, boundary_cells.shape[0]), jnp.int32),
            vmem((1, boundary_source.shape[0]), jnp.int32),
            vmem(series.shape, f32),
            vmem((1, blocks), jnp.int32),
            vmem((tall, width), f32),
            vmem((n, tall, width), f32),
            vmem((blocks, wide), f32),
            vmem((3, wide, wide), bf16),
            vmem((3, wide, wide), bf16),
            vmem((2, wide, wide), bf16),
            vmem((2, 4 * cells, wide), bf16),
            vmem((2, 4 * cells, wide), bf16),
            vmem((2, wide, wide), bf16),
            vmem((2, cells, wide), bf16),
            vmem((steps, blocks, wide), f32),
            vmem((blocks, cells), f32),
            vmem((3 * blocks, blocks), bf16),
            vmem((blocks, 3 * blocks), bf16),
            vmem((blocks, cells), f32),
            vmem((blocks, wide), f32),
            vmem((steps, blocks, cells), f32),
            vmem((blocks, cells), f32),
            vmem((steps, 2, half, cells), f32),
            vmem((steps, 2, half, cells), f32),
            vmem((steps + 1, blocks, cells), f32),
            vmem((steps, 2, half, cells), f32),
            vmem((n * slots, blocks), bf16),
            vmem((n, slots, cells), f32),
            vmem((n, slots, wide), f32),
            dma((12,)),
            dma,
            dma,
            dma((steps, 2, 2)),
            dma((steps, 2, 2)),
            dma((steps, 2, 2)),
            dma((steps, 2, 2)),
            dma((2,)),
            dma((2,)),
            dma((2,)),
        ],
        compiler_params=pltpu.CompilerParams(
            collective_id=0, has_side_effects=True, vmem_limit_bytes=60 * 1024 * 1024
        ),
        name="surge",
    )(
        elevation,
        momentum.reshape(2 * blocks, cells),
        depth,
        drag,
        div_weight.reshape(5 * wide, cells),
        grad_weight.reshape(5 * cells, wide),
        neighbours.T,
        wet,
        boundary_cells.reshape(1, -1),
        boundary_source.reshape(1, -1),
        series,
        moved_from.reshape(1, -1),
    )
    level, flow = pl.pallas_call(
        functools.partial(settle, slots),
        out_shape=(
            jax.ShapeDtypeStruct((blocks, cells), f32),
            jax.ShapeDtypeStruct((2 * blocks, cells), f32),
        ),
        in_specs=[pl.BlockSpec(memory_space=vmem)] * 3,
        out_specs=(pl.BlockSpec(memory_space=vmem),) * 2,
        compiler_params=pltpu.CompilerParams(vmem_limit_bytes=60 * 1024 * 1024),
        name="settle",
    )(
        moved_from.reshape(1, -1),
        landed_level.reshape(n * slots, cells),
        landed_flow.reshape(n * slots, wide),
    )
    return level, flow.reshape(blocks, 2, cells)


def solution(mesh):
    n = mesh.shape["dom"]
    return jax.shard_map(
        functools.partial(local, n),
        mesh=mesh,
        in_specs=(
            P("dom", None),
            P("dom", None, None),
            P("dom", None),
            P("dom", None),
            P(),
            P(),
            P("dom", None),
            P(None, "dom"),
            P("dom"),
            P("dom"),
            P(None, "dom"),
            P("dom"),
        ),
        out_specs=(P("dom", None), P("dom", None, None)),
        check_vma=False,
    )
```

```python
import functools

import jax
import jax.numpy as jnp
from jax import lax
from jax.experimental import pallas as pl
from jax.experimental.pallas import tpu as pltpu
from jax.sharding import PartitionSpec as P

MESH = pl.DeviceIdType.MESH
f32 = jnp.float32
bf16 = jnp.bfloat16
relax_rate = 0.5


def halves(x):
    hi = x.astype(bf16)
    return hi, (x - hi.astype(f32)).astype(bf16)


def mm(a, b):
    return jnp.dot(a, b, preferred_element_type=f32)


def mm3(hi, lo, w_hi, w_lo):
    return mm(hi, w_hi) + (mm(lo, w_hi) + mm(hi, w_lo))


def hot(cond):
    return jnp.where(cond, 1.0, 0.0).astype(f32)


def iota(shape, dim):
    return lax.broadcasted_iota(jnp.int32, shape, dim).astype(f32)


def kernel(
    n, slots,
    elev_hbm, mom_hbm, depth_hbm, drag_hbm, divw_hbm, gradw_hbm, nb_hbm, wet_hbm,
    cells_hbm, source_hbm, series_hbm, moved_hbm,
    landed_level, landed_flow,
    elev_ref, mom_ref, depth_ref, drag_ref, divw_ref, gradw_ref, nb_ref, wet_ref,
    cells_ref, source_ref, series_ref, moved_ref,
    meta, gathered, x_ref, dl_hi, dl_lo, ds_both, gl_hi, gl_lo, gs_twice, gs_lo,
    damp_ref, depth_p, near_rows, near_cols, div_ref, grad_ref,
    force_ref, relax_ref, div_send, div_recv, lev_send, lev_recv, pack, packed_level, packed_flow,
    in_ss, meta_ss, meta_rs, div_ss, div_rs, lev_ss, lev_rs, mig_ss, mig_rs, own_ss,
):
    me = lax.axis_index("dom")
    steps, width = series_ref.shape
    blocks, cells = elev_ref.shape
    half = blocks // 2
    wide = 2 * cells
    span = blocks // width

    inputs = [
        pltpu.make_async_copy(src, dst, in_ss.at[i])
        for i, (src, dst) in enumerate(
            (
                (nb_hbm, nb_ref),
                (moved_hbm, moved_ref),
                (series_hbm, series_ref),
                (wet_hbm, wet_ref),
                (cells_hbm, cells_ref),
                (source_hbm, source_ref),
                (mom_hbm, mom_ref),
                (elev_hbm, elev_ref),
                (depth_hbm, depth_ref),
                (drag_hbm, drag_ref),
                (divw_hbm, divw_ref),
                (gradw_hbm, gradw_ref),
            )
        )
    ]
    for copy in inputs:
        copy.start()

    barrier = pltpu.get_barrier_semaphore()

    def greet(i, _):
        pl.semaphore_signal(
            barrier, inc=1, device_id=(lax.rem(me + i, n),), device_id_type=MESH
        )
        return 0

    lax.fori_loop(1, n, greet, 0)

    bits = n.bit_length() - 1
    flips = [(1 - 2 * lax.rem(lax.div(me, 1 << k), 2)) * (1 << k) for k in range(bits)]

    def partner(i):
        j = i - 1
        m = lax.div(j + 1, 2) + (1 - lax.rem(j, 2)) * (n // 2)
        if n != 1 << bits:
            return lax.rem(me + m, n)
        return me + sum(lax.rem(lax.div(m, 1 << k), 2) * flips[k] for k in range(bits))

    def sl(k, size):
        return slice(k * size, (k + 1) * size)

    near_half, far_half = 1 - lax.rem(me, 2), lax.rem(me, 2)

    near_pieces = [(near_half, 0, 0, half)]
    far_pieces = [(far_half, i, i * (half // 2), half // 2) for i in (0, 1)]

    def rows_of(piece):
        h, _, first, size = piece
        return pl.ds(pl.multiple_of(h * half + first, half // 2), size)

    for copy in inputs[:6]:
        copy.wait()
    base = (me * blocks).astype(f32)
    square = (blocks, blocks)
    sub, lane = iota(square, 0), iota(square, 1)
    nb = nb_ref[...].astype(f32)
    nbl = nb - base
    lower_own = jnp.logical_and(nbl[2:3] >= 0.0, nbl[2:3] < float(blocks))
    key_row = jnp.where(lower_own, nb[3:4] + float(blocks), lane[0:1])
    key_col = jnp.sum(jnp.where(sub == lane, key_row, 0.0), axis=1, keepdims=True)
    pos_row = jnp.sum(hot(key_col < key_row), axis=0, keepdims=True)
    pos_col = jnp.sum(hot(key_row < key_col), axis=1, keepdims=True)
    order = hot(sub == pos_row)
    order16 = order.astype(bf16)

    for copy in inputs[6:10]:
        copy.wait()
    field = jnp.concatenate(
        [
            mom_ref[pl.ds(0, blocks, 2), :],
            mom_ref[pl.ds(1, blocks, 2), :],
            elev_ref[...],
            depth_ref[...],
            drag_ref[...],
        ],
        axis=1,
    )
    hi, lo = halves(field)
    field = mm(order16, hi) + mm(order16, lo)
    x_ref[...] = field[:, :wide]
    elevation0 = field[:, wide : 3 * cells]
    depth_p[...] = field[:, 3 * cells : 4 * cells]
    damping = 1.0 / (1.0 + field[:, 4 * cells :])
    inputs[10].wait()
    hi, lo = halves(divw_ref[...])
    for half_w, local_w in ((hi, dl_hi), (lo, dl_lo)):
        slot = [half_w[sl(k, wide), :] for k in range(5)]
        local_w[0] = jnp.concatenate([slot[0], slot[1]], axis=1)
        for h in (0, 1):
            local_w[1 + h] = jnp.concatenate([slot[2], slot[3 + h]], axis=1)
    for h in (0, 1):
        ds_both[h] = jnp.concatenate([hi[sl(4 - h, wide), :], lo[sl(4 - h, wide), :]], axis=1)

    def halo(src, recv, ss, rs, step, piece):
        h, i, first, size = piece
        return pltpu.make_async_remote_copy(
            src_ref=src,
            dst_ref=recv.at[step, 1 - h, pl.ds(first, size)],
            send_sem=ss.at[step, h, i],
            recv_sem=rs.at[step, 1 - h, i],
            device_id=(lax.rem(me + 2 * h - 1 + n, n),),
            device_id_type=MESH,
        )

    def div_copy(step, piece):
        h, _, first, size = piece
        src = div_send.at[step, h, pl.ds(first, size)]
        return halo(src, div_recv, div_ss, div_rs, step, piece)

    def lev_copy(step, piece):
        src = lev_send.at[step + 1, rows_of(piece)]
        return halo(src, lev_recv, lev_ss, lev_rs, step, piece)

    def facing(piece):
        return (1 - piece[0],) + piece[1:]

    def shed(step, piece):
        h, _, first, size = piece
        hi, lo = halves(x_ref[rows_of(piece), :])
        both = mm(hi, ds_both[h])
        rest = mm(lo, ds_both[h, :, :cells])
        div_send[step, h, first : first + size] = both[:, :cells] + (both[:, cells:] + rest)

    def tile_copy(target, source):
        return pltpu.make_async_remote_copy(
            src_ref=meta,
            dst_ref=gathered.at[source],
            send_sem=meta_ss,
            recv_sem=meta_rs,
            device_id=(target,),
            device_id_type=MESH,
        )

    def state_copy(kind, target, source):
        src, dst = ((packed_level, landed_level), (packed_flow, landed_flow))[kind]
        return pltpu.make_async_remote_copy(
            src_ref=src.at[target],
            dst_ref=dst.at[source],
            send_sem=mig_ss.at[kind],
            recv_sem=mig_rs.at[kind],
            device_id=(target,),
            device_id_type=MESH,
        )

    def all_done(ref, sem):
        others = ref.at[pl.ds(0, n - 1)]
        pltpu.make_async_copy(others, others, sem).wait()

    def own_copy(kind):
        src, dst = ((packed_level, landed_level), (packed_flow, landed_flow))[kind]
        return pltpu.make_async_copy(src.at[me], dst.at[me], own_ss.at[kind])

    def migrate(kind, hi, lo):
        src = (packed_level, packed_flow)[kind]
        src[...] = (mm(pack[...], hi) + mm(pack[...], lo)).reshape(src.shape)

        def send(i, _):
            state_copy(kind, partner(i), me).start()
            return 0

        lax.fori_loop(1, n, send, 0)
        own_copy(kind).start()

    moved = moved_ref[...].astype(f32)

    def open_up():
        meta[...] = jnp.zeros_like(meta)
        meta[0:steps, :] = series_ref[...]
        for i in range(span):
            meta[steps + i : steps + i + 1, :] = moved[:, i * width : (i + 1) * width]
        gathered[pl.ds(me, 1)] = meta[...][None]
        pl.semaphore_wait(barrier, n - 1)

    def send_tiles():
        def send(i, _):
            tile_copy(partner(i), me).start()
            return 0

        lax.fori_loop(1, n, send, 0)

        def place(ids):
            return jnp.sum(jnp.where(sub == ids, pos_col, 0.0), axis=0, keepdims=True)

        vertical = jnp.where(lower_own, nbl[2:3], nbl[3:4])
        for k, ids in enumerate((nbl[0:1], nbl[1:2], vertical)):
            col = jnp.sum(order * place(ids), axis=1, keepdims=True)
            near = hot(lane == col).astype(bf16)
            near_rows[sl(k, blocks), :] = near
            near_cols[:, sl(k, blocks)] = near
        wet = wet_ref[...].astype(f32)
        for s in range(steps):
            mask = jnp.sum(order * wet[s : s + 1], axis=1, keepdims=True)
            damp_ref[s, :, :cells] = jnp.broadcast_to(mask, (blocks, cells))
            damp_ref[s, :, cells:] = mask * damping

    def boundary():
        entries = cells_ref.shape[1]
        point = source_ref[...].astype(f32)
        chunk = jnp.floor((point + 0.5) * (1.0 / width))
        spot = point - chunk * width
        pick = hot(iota((width, entries), 0) == spot).astype(bf16)
        cell = cells_ref[...].astype(f32)
        block = jnp.floor((cell + 0.5) * (1.0 / cells))
        element = cell - block * cells
        block_place = jnp.sum(
            jnp.where(iota((blocks, entries), 0) == block, pos_col, 0.0), axis=0, keepdims=True
        )
        rows = hot(iota((blocks, entries), 0) == block_place).astype(bf16)
        columns = hot(iota((cells, entries), 0) == element)

        def spread(values):
            return lax.dot_general(
                rows, values, (((1,), (1,)), ((), ())), preferred_element_type=f32
            )

        relax_ref[...] = relax_rate * spread(columns.astype(bf16))

        all_done(gathered, meta_rs)
        tall = meta.shape[0]
        hi, lo = halves(gathered[...].reshape(n * tall, width))
        found = (mm(hi, pick) + mm(lo, pick)).reshape(n, tall, entries)
        found = jnp.sum(jnp.where(iota(found.shape, 0) == chunk[None], found, 0.0), axis=0)

        def force(s):
            hi, lo = halves(columns * found[s : s + 1])
            force_ref[s] = spread(hi) + spread(lo)

        force(0)
        return force

    def choose():
        everyone = gathered[...]
        takes = jnp.concatenate([everyone[:, steps + i, :] for i in range(span)], axis=1) - base
        mine = hot(jnp.logical_and(takes >= 0.0, takes < float(blocks)))
        rank = mm(mine.astype(bf16), hot(sub < lane).astype(bf16))
        rank = jnp.where(mine > 0.0, rank, -1.0)
        cube = (n, slots, blocks)
        chosen = jnp.where(rank[:, None, :] == iota(cube, 1), takes[:, None, :] + 1.0, 0.0)
        chosen = jnp.sum(chosen.reshape(n * slots, blocks), axis=1, keepdims=True) - 1.0
        lanes = iota((n * slots, blocks), 1)
        pack[...] = mm(
            hot(lanes == chosen).astype(bf16), hot(lane == pos_col).astype(bf16)
        ).astype(bf16)

    def one_step(step, opening, closing):
        if opening:
            open_up()
            for piece in far_pieces + near_pieces:
                div_copy(step, piece).start()
            send_tiles()
        hi, lo = halves(x_ref[...])
        first = mm3(hi, lo, dl_hi[0], dl_lo[0])
        second = jnp.concatenate(
            [
                mm3(hi[sl(h, half)], lo[sl(h, half)], dl_hi[1 + h], dl_lo[1 + h])
                for h in (0, 1)
            ],
            axis=0,
        )
        parts = jnp.concatenate([first[:, cells:], second[:, :cells], second[:, cells:]], axis=0)
        parts = mm(near_cols[...], jnp.concatenate(halves(parts), axis=1))
        div_ref[...] = first[:, :cells] + (parts[:, :cells] + parts[:, cells:])
        if opening:
            force = boundary()
        for piece in near_pieces + far_pieces:
            h, _, first, size = piece
            r = rows_of(piece)
            div_copy(step, facing(piece)).wait_recv()
            div = div_ref[r, :] + div_recv[step, h, first : first + size]
            level = lev_send[step, r, :] - damp_ref[step, r, :cells] * div
            lev_send[step + 1, r, :] = level + relax_ref[r, :] * (force_ref[step, r, :] - level)
            lev_copy(step, piece).start()
        if opening:
            inputs[11].wait()
            hi, lo = halves(gradw_ref[...])
            for half_w, local_w in ((hi, gl_hi), (lo, gl_lo)):
                slot = [half_w[sl(k, cells), :] for k in range(5)]
                for h in (0, 1):
                    local_w[h] = jnp.concatenate(slot[:3] + [slot[4 - h]], axis=0)
            for h in (0, 1):
                gs_twice[h] = jnp.concatenate([hi[sl(3 + h, cells), :]] * 2, axis=0)
                gs_lo[h] = lo[sl(3 + h, cells), :]
        hi, lo = halves(lev_send[step + 1])
        if closing:
            migrate(0, hi, lo)
        near = mm(near_rows[...], jnp.concatenate([hi, lo], axis=1)).astype(bf16)
        near = [near[sl(k, blocks)] for k in range(3)]
        hi4 = jnp.concatenate([hi] + [p[:, :cells] for p in near], axis=1)
        lo4 = jnp.concatenate([lo] + [p[:, cells:] for p in near], axis=1)
        for h in (0, 1):
            r = sl(h, half)
            grad_ref[r, :] = mm3(hi4[r], lo4[r], gl_hi[h], gl_lo[h])
        if opening:
            for later in range(1, steps):
                force(later)
            choose()
        for piece in near_pieces + far_pieces:
            h, _, first, size = piece
            r = rows_of(piece)
            lev_copy(step, facing(piece)).wait_recv()
            hi, lo = halves(lev_recv[step, h, first : first + size])
            grad = mm(jnp.concatenate([hi, lo], axis=1), gs_twice[h]) + mm(hi, gs_lo[h])
            grad = grad_ref[r, :] + grad
            depth = depth_p[r, :]
            damp = damp_ref[step, r, cells:]
            x_ref[r, :cells] = damp * (x_ref[r, :cells] - depth * grad[:, :cells])
            x_ref[r, cells:] = damp * (x_ref[r, cells:] - depth * grad[:, cells:])
            if not closing:
                shed(step + 1, piece)
                div_copy(step + 1, piece).start()

    lev_send[0] = elevation0
    for piece in far_pieces + near_pieces:
        shed(0, piece)
    one_step(0, True, False)

    def middle(step, _):
        one_step(step, False, False)
        return 0

    lax.fori_loop(1, steps - 1, middle, 0)
    one_step(steps - 1, False, True)
    migrate(1, *halves(x_ref[...]))

    def halo_sent(step, _):
        for piece in near_pieces + far_pieces:
            div_copy(step, piece).wait_send()
            lev_copy(step, piece).wait_send()
        return 0

    lax.fori_loop(0, steps, halo_sent, 0)
    all_done(gathered, meta_ss)
    for kind, src, dst in ((0, packed_level, landed_level), (1, packed_flow, landed_flow)):
        own_copy(kind).wait()
        all_done(src, mig_ss.at[kind])
        all_done(dst, mig_rs.at[kind])


def settle(
    slots, moved_hbm, level_hbm, flow_hbm, level_out, flow_out,
    moved_ref, landed_level, landed_flow, level_ref, flow_ref, sem,
):
    copies = [
        pltpu.make_async_copy(src, dst, sem.at[i])
        for i, (src, dst) in enumerate(
            (
                (moved_hbm, moved_ref),
                (level_hbm, landed_level),
                (flow_hbm, landed_flow),
                (level_ref, level_out),
                (flow_ref, flow_out),
            )
        )
    ]
    for copy in copies[:3]:
        copy.start()
    blocks, cells = level_ref.shape
    places = landed_level.shape[0]
    square = (blocks, blocks)
    sub, lane = iota(square, 0), iota(square, 1)
    copies[0].wait()
    owner_row = jnp.floor((moved_ref[...].astype(f32) + 0.5) * (1.0 / blocks))
    owner_col = jnp.sum(jnp.where(sub == lane, owner_row, 0.0), axis=1, keepdims=True)
    ahead = jnp.sum(
        jnp.where(lane < sub, hot(owner_row == owner_col), 0.0), axis=1, keepdims=True
    )
    where_from = owner_col * float(slots) + ahead
    unpack = hot(iota((blocks, places), 1) == where_from).astype(bf16)
    copies[1].wait()
    hi, lo = halves(landed_level[...])
    both = mm(unpack, jnp.concatenate([hi, lo], axis=1))
    level_ref[...] = both[:, :cells] + both[:, cells:]
    copies[3].start()
    copies[2].wait()
    hi, lo = halves(landed_flow[...])
    flow = mm(unpack, hi) + mm(unpack, lo)
    flow_ref[pl.ds(0, blocks, 2), :] = flow[:, :cells]
    flow_ref[pl.ds(1, blocks, 2), :] = flow[:, cells:]
    copies[4].start()
    copies[3].wait()
    copies[4].wait()


def local(
    n,
    elevation,
    momentum,
    depth,
    drag,
    div_weight,
    grad_weight,
    neighbours,
    wet,
    boundary_cells,
    boundary_source,
    series,
    moved_from,
):
    blocks, cells = elevation.shape
    steps, width = series.shape
    half = blocks // 2
    wide = 2 * cells
    portion = 2 * blocks // n
    slots = -(-portion // 8) * 8
    tall = -(-(steps + blocks // width) // 8) * 8
    vmem, dma = pltpu.VMEM, pltpu.SemaphoreType.DMA
    landed_level, landed_flow = pl.pallas_call(
        functools.partial(kernel, n, slots),
        out_shape=(
            jax.ShapeDtypeStruct((n, slots, cells), f32),
            jax.ShapeDtypeStruct((n, slots, wide), f32),
        ),
        in_specs=[pl.BlockSpec(memory_space=pl.ANY)] * 12,
        out_specs=(pl.BlockSpec(memory_space=pl.ANY),) * 2,
        scratch_shapes=[
            vmem((blocks, cells), f32),
            vmem((2 * blocks, cells), f32),
            vmem((blocks, cells), f32),
            vmem((blocks, cells), f32),
            vmem((5 * wide, cells), f32),
            vmem((5 * cells, wide), f32),
            vmem((4, blocks), jnp.int32),
            vmem(wet.shape, jnp.int32),
            vmem((1, boundary_cells.shape[0]), jnp.int32),
            vmem((1, boundary_source.shape[0]), jnp.int32),
            vmem(series.shape, f32),
            vmem((1, blocks), jnp.int32),
            vmem((tall, width), f32),
            vmem((n, tall, width), f32),
            vmem((blocks, wide), f32),
            vmem((3, wide, wide), bf16),
            vmem((3, wide, wide), bf16),
            vmem((2, wide, wide), bf16),
            vmem((2, 4 * cells, wide), bf16),
            vmem((2, 4 * cells, wide), bf16),
            vmem((2, wide, wide), bf16),
            vmem((2, cells, wide), bf16),
            vmem((steps, blocks, wide), f32),
            vmem((blocks, cells), f32),
            vmem((3 * blocks, blocks), bf16),
            vmem((blocks, 3 * blocks), bf16),
            vmem((blocks, cells), f32),
            vmem((blocks, wide), f32),
            vmem((steps, blocks, cells), f32),
            vmem((blocks, cells), f32),
            vmem((steps, 2, half, cells), f32),
            vmem((steps, 2, half, cells), f32),
            vmem((steps + 1, blocks, cells), f32),
            vmem((steps, 2, half, cells), f32),
            vmem((n * slots, blocks), bf16),
            vmem((n, slots, cells), f32),
            vmem((n, slots, wide), f32),
            dma((12,)),
            dma,
            dma,
            dma((steps, 2, 2)),
            dma((steps, 2, 2)),
            dma((steps, 2, 2)),
            dma((steps, 2, 2)),
            dma((2,)),
            dma((2,)),
            dma((2,)),
        ],
        compiler_params=pltpu.CompilerParams(
            collective_id=0, has_side_effects=True, vmem_limit_bytes=60 * 1024 * 1024
        ),
        name="surge",
    )(
        elevation,
        momentum.reshape(2 * blocks, cells),
        depth,
        drag,
        div_weight.reshape(5 * wide, cells),
        grad_weight.reshape(5 * cells, wide),
        neighbours.T,
        wet,
        boundary_cells.reshape(1, -1),
        boundary_source.reshape(1, -1),
        series,
        moved_from.reshape(1, -1),
    )
    level, flow = pl.pallas_call(
        functools.partial(settle, slots),
        out_shape=(
            jax.ShapeDtypeStruct((blocks, cells), f32),
            jax.ShapeDtypeStruct((2 * blocks, cells), f32),
        ),
        in_specs=[pl.BlockSpec(memory_space=pl.ANY)] * 3,
        out_specs=(pl.BlockSpec(memory_space=pl.ANY),) * 2,
        scratch_shapes=[
            vmem((1, blocks), jnp.int32),
            vmem((n * slots, cells), f32),
            vmem((n * slots, wide), f32),
            vmem((blocks, cells), f32),
            vmem((2 * blocks, cells), f32),
            dma((5,)),
        ],
        compiler_params=pltpu.CompilerParams(vmem_limit_bytes=60 * 1024 * 1024),
        name="settle",
    )(
        moved_from.reshape(1, -1),
        landed_level.reshape(n * slots, cells),
        landed_flow.reshape(n * slots, wide),
    )
    return level, flow.reshape(blocks, 2, cells)


def solution(mesh):
    n = mesh.shape["dom"]
    return jax.shard_map(
        functools.partial(local, n),
        mesh=mesh,
        in_specs=(
            P("dom", None),
            P("dom", None, None),
            P("dom", None),
            P("dom", None),
            P(),
            P(),
            P("dom", None),
            P(None, "dom"),
            P("dom"),
            P("dom"),
            P(None, "dom"),
            P("dom"),
        ),
        out_specs=(P("dom", None), P("dom", None, None)),
        check_vma=False,
    )
```

```python
import functools

import jax
import jax.numpy as jnp
from jax import lax
from jax.experimental import pallas as pl
from jax.experimental.pallas import tpu as pltpu
from jax.sharding import PartitionSpec as P

MESH = pl.DeviceIdType.MESH
f32 = jnp.float32
bf16 = jnp.bfloat16
relax_rate = 0.5


def halves(x):
    hi = x.astype(bf16)
    return hi, (x - hi.astype(f32)).astype(bf16)


def mm(a, b):
    return jnp.dot(a, b, preferred_element_type=f32)


def mm3(hi, lo, w_hi, w_lo):
    return mm(hi, w_hi) + (mm(lo, w_hi) + mm(hi, w_lo))


def hot(cond):
    return jnp.where(cond, 1.0, 0.0).astype(f32)


def iota(shape, dim):
    return lax.broadcasted_iota(jnp.int32, shape, dim).astype(f32)


def kernel(
    n, slots,
    elev_hbm, mom_hbm, depth_hbm, drag_hbm, divw_hbm, gradw_hbm, nb_hbm, wet_hbm,
    cells_hbm, source_hbm, series_hbm, moved_hbm,
    landed_level, landed_flow,
    elev_ref, mom_ref, depth_ref, drag_ref, divw_ref, gradw_ref, nb_ref, wet_ref,
    cells_ref, source_ref, series_ref, moved_ref,
    meta, gathered, x_ref, dl_hi, dl_lo, ds_both, gl_hi, gl_lo, gs_twice, gs_lo,
    damp_ref, depth_p, near_rows, near_cols, div_ref, grad_ref,
    force_ref, relax_ref, div_send, div_recv, lev_send, lev_recv, pack, packed_level, packed_flow,
    in_ss, meta_ss, meta_rs, div_ss, div_rs, lev_ss, lev_rs, mig_ss, mig_rs, own_ss,
):
    me = lax.axis_index("dom")
    steps, width = series_ref.shape
    blocks, cells = elev_ref.shape
    half = blocks // 2
    wide = 2 * cells
    span = blocks // width

    inputs = [
        pltpu.make_async_copy(src, dst, in_ss.at[i])
        for i, (src, dst) in enumerate(
            (
                (nb_hbm, nb_ref),
                (moved_hbm, moved_ref),
                (series_hbm, series_ref),
                (wet_hbm, wet_ref),
                (cells_hbm, cells_ref),
                (source_hbm, source_ref),
                (mom_hbm, mom_ref),
                (elev_hbm, elev_ref),
                (depth_hbm, depth_ref),
                (drag_hbm, drag_ref),
                (divw_hbm, divw_ref),
                (gradw_hbm, gradw_ref),
            )
        )
    ]
    for copy in inputs:
        copy.start()

    barrier = pltpu.get_barrier_semaphore()

    def greet(i, _):
        pl.semaphore_signal(
            barrier, inc=1, device_id=(lax.rem(me + i, n),), device_id_type=MESH
        )
        return 0

    lax.fori_loop(1, n, greet, 0)

    bits = n.bit_length() - 1
    flips = [(1 - 2 * lax.rem(lax.div(me, 1 << k), 2)) * (1 << k) for k in range(bits)]

    def partner(i):
        j = i - 1
        m = lax.div(j + 1, 2) + (1 - lax.rem(j, 2)) * (n // 2)
        if n != 1 << bits:
            return lax.rem(me + m, n)
        return me + sum(lax.rem(lax.div(m, 1 << k), 2) * flips[k] for k in range(bits))

    def sl(k, size):
        return slice(k * size, (k + 1) * size)

    near_half, far_half = 1 - lax.rem(me, 2), lax.rem(me, 2)

    near_pieces = [(near_half, 0, 0, half)]
    far_pieces = [(far_half, i, i * (half // 2), half // 2) for i in (0, 1)]

    def rows_of(piece):
        h, _, first, size = piece
        return pl.ds(pl.multiple_of(h * half + first, half // 2), size)

    for copy in inputs[:6]:
        copy.wait()
    base = (me * blocks).astype(f32)
    square = (blocks, blocks)
    sub, lane = iota(square, 0), iota(square, 1)
    nb = nb_ref[...].astype(f32)
    nbl = nb - base
    lower_own = jnp.logical_and(nbl[2:3] >= 0.0, nbl[2:3] < float(blocks))
    key_row = jnp.where(lower_own, nb[3:4] + float(blocks), lane[0:1])
    key_col = jnp.sum(jnp.where(sub == lane, key_row, 0.0), axis=1, keepdims=True)
    pos_row = jnp.sum(hot(key_col < key_row), axis=0, keepdims=True)
    pos_col = jnp.sum(hot(key_row < key_col), axis=1, keepdims=True)
    order = hot(sub == pos_row)
    order16 = order.astype(bf16)

    inputs[6].wait()
    hi, lo = halves(
        jnp.concatenate(
            [mom_ref[pl.ds(0, blocks, 2), :], mom_ref[pl.ds(1, blocks, 2), :]], axis=1
        )
    )
    x_ref[...] = mm(order16, hi) + mm(order16, lo)
    inputs[10].wait()
    for h in (0, 1):
        hi, lo = halves(divw_ref[sl(4 - h, wide), :])
        ds_both[h] = jnp.concatenate([hi, lo], axis=1)

    def halo(src, recv, ss, rs, step, piece):
        h, i, first, size = piece
        return pltpu.make_async_remote_copy(
            src_ref=src,
            dst_ref=recv.at[step, 1 - h, pl.ds(first, size)],
            send_sem=ss.at[step, h, i],
            recv_sem=rs.at[step, 1 - h, i],
            device_id=(lax.rem(me + 2 * h - 1 + n, n),),
            device_id_type=MESH,
        )

    def div_copy(step, piece):
        h, _, first, size = piece
        src = div_send.at[step, h, pl.ds(first, size)]
        return halo(src, div_recv, div_ss, div_rs, step, piece)

    def lev_copy(step, piece):
        src = lev_send.at[step + 1, rows_of(piece)]
        return halo(src, lev_recv, lev_ss, lev_rs, step, piece)

    def facing(piece):
        return (1 - piece[0],) + piece[1:]

    def shed(step, piece):
        h, _, first, size = piece
        hi, lo = halves(x_ref[rows_of(piece), :])
        both = mm(hi, ds_both[h])
        rest = mm(lo, ds_both[h, :, :cells])
        div_send[step, h, first : first + size] = both[:, :cells] + (both[:, cells:] + rest)

    def tile_copy(target, source):
        return pltpu.make_async_remote_copy(
            src_ref=meta,
            dst_ref=gathered.at[source],
            send_sem=meta_ss,
            recv_sem=meta_rs,
            device_id=(target,),
            device_id_type=MESH,
        )

    def state_copy(kind, target, source):
        src, dst = ((packed_level, landed_level), (packed_flow, landed_flow))[kind]
        return pltpu.make_async_remote_copy(
            src_ref=src.at[target],
            dst_ref=dst.at[source],
            send_sem=mig_ss.at[kind],
            recv_sem=mig_rs.at[kind],
            device_id=(target,),
            device_id_type=MESH,
        )

    def all_done(ref, sem):
        others = ref.at[pl.ds(0, n - 1)]
        pltpu.make_async_copy(others, others, sem).wait()

    def own_copy(kind):
        src, dst = ((packed_level, landed_level), (packed_flow, landed_flow))[kind]
        return pltpu.make_async_copy(src.at[me], dst.at[me], own_ss.at[kind])

    def migrate(kind, hi, lo):
        src = (packed_level, packed_flow)[kind]
        src[...] = (mm(pack[...], hi) + mm(pack[...], lo)).reshape(src.shape)

        def send(i, _):
            state_copy(kind, partner(i), me).start()
            return 0

        lax.fori_loop(1, n, send, 0)
        own_copy(kind).start()

    moved = moved_ref[...].astype(f32)

    def open_up():
        meta[...] = jnp.zeros_like(meta)
        meta[0:steps, :] = series_ref[...]
        for i in range(span):
            meta[steps + i : steps + i + 1, :] = moved[:, i * width : (i + 1) * width]
        gathered[pl.ds(me, 1)] = meta[...][None]
        pl.semaphore_wait(barrier, n - 1)

    def send_tiles():
        def send(i, _):
            tile_copy(partner(i), me).start()
            return 0

        lax.fori_loop(1, n, send, 0)

        def place(ids):
            return jnp.sum(jnp.where(sub == ids, pos_col, 0.0), axis=0, keepdims=True)

        vertical = jnp.where(lower_own, nbl[2:3], nbl[3:4])
        for k, ids in enumerate((nbl[0:1], nbl[1:2], vertical)):
            col = jnp.sum(order * place(ids), axis=1, keepdims=True)
            near = hot(lane == col).astype(bf16)
            near_rows[sl(k, blocks), :] = near
            near_cols[:, sl(k, blocks)] = near
        for copy in inputs[7:10]:
            copy.wait()
        hi, lo = halves(jnp.concatenate([elev_ref[...], depth_ref[...], drag_ref[...]], axis=1))
        field = mm(order16, hi) + mm(order16, lo)
        lev_send[0] = field[:, :cells]
        depth_p[...] = field[:, cells : 2 * cells]
        damping = 1.0 / (1.0 + field[:, 2 * cells :])
        hi, lo = halves(divw_ref[...])
        for half_w, local_w in ((hi, dl_hi), (lo, dl_lo)):
            slot = [half_w[sl(k, wide), :] for k in range(5)]
            local_w[0] = jnp.concatenate([slot[0], slot[1]], axis=1)
            for h in (0, 1):
                local_w[1 + h] = jnp.concatenate([slot[2], slot[3 + h]], axis=1)
        wet = wet_ref[...].astype(f32)
        for s in range(steps):
            mask = jnp.sum(order * wet[s : s + 1], axis=1, keepdims=True)
            damp_ref[s, :, :cells] = jnp.broadcast_to(mask, (blocks, cells))
            damp_ref[s, :, cells:] = mask * damping

    def boundary():
        entries = cells_ref.shape[1]
        point = source_ref[...].astype(f32)
        chunk = jnp.floor((point + 0.5) * (1.0 / width))
        spot = point - chunk * width
        pick = hot(iota((width, entries), 0) == spot).astype(bf16)
        cell = cells_ref[...].astype(f32)
        block = jnp.floor((cell + 0.5) * (1.0 / cells))
        element = cell - block * cells
        block_place = jnp.sum(
            jnp.where(iota((blocks, entries), 0) == block, pos_col, 0.0), axis=0, keepdims=True
        )
        rows = hot(iota((blocks, entries), 0) == block_place).astype(bf16)
        columns = hot(iota((cells, entries), 0) == element)

        def spread(values):
            return lax.dot_general(
                rows, values, (((1,), (1,)), ((), ())), preferred_element_type=f32
            )

        relax_ref[...] = relax_rate * spread(columns.astype(bf16))

        all_done(gathered, meta_rs)
        tall = meta.shape[0]
        hi, lo = halves(gathered[...].reshape(n * tall, width))
        found = (mm(hi, pick) + mm(lo, pick)).reshape(n, tall, entries)
        found = jnp.sum(jnp.where(iota(found.shape, 0) == chunk[None], found, 0.0), axis=0)

        def force(s):
            hi, lo = halves(columns * found[s : s + 1])
            force_ref[s] = spread(hi) + spread(lo)

        force(0)
        return force

    def choose():
        everyone = gathered[...]
        takes = jnp.concatenate([everyone[:, steps + i, :] for i in range(span)], axis=1) - base
        mine = hot(jnp.logical_and(takes >= 0.0, takes < float(blocks)))
        rank = mm(mine.astype(bf16), hot(sub < lane).astype(bf16))
        rank = jnp.where(mine > 0.0, rank, -1.0)
        cube = (n, slots, blocks)
        chosen = jnp.where(rank[:, None, :] == iota(cube, 1), takes[:, None, :] + 1.0, 0.0)
        chosen = jnp.sum(chosen.reshape(n * slots, blocks), axis=1, keepdims=True) - 1.0
        lanes = iota((n * slots, blocks), 1)
        pack[...] = mm(
            hot(lanes == chosen).astype(bf16), hot(lane == pos_col).astype(bf16)
        ).astype(bf16)

    def one_step(step):
        opening, closing = step == 0, step == steps - 1

        @pl.when(opening)
        def _():
            open_up()
            for piece in far_pieces + near_pieces:
                div_copy(step, piece).start()
            send_tiles()
        hi, lo = halves(x_ref[...])
        first = mm3(hi, lo, dl_hi[0], dl_lo[0])
        second = jnp.concatenate(
            [
                mm3(hi[sl(h, half)], lo[sl(h, half)], dl_hi[1 + h], dl_lo[1 + h])
                for h in (0, 1)
            ],
            axis=0,
        )
        parts = jnp.concatenate([first[:, cells:], second[:, :cells], second[:, cells:]], axis=0)
        parts = mm(near_cols[...], jnp.concatenate(halves(parts), axis=1))
        div_ref[...] = first[:, :cells] + (parts[:, :cells] + parts[:, cells:])
        @pl.when(opening)
        def _():
            force = boundary()
            for later in range(1, steps):
                force(later)

        for piece in near_pieces + far_pieces:
            h, _, first, size = piece
            r = rows_of(piece)
            div_copy(step, facing(piece)).wait_recv()
            div = div_ref[r, :] + div_recv[step, h, first : first + size]
            level = lev_send[step, r, :] - damp_ref[step, r, :cells] * div
            lev_send[step + 1, r, :] = level + relax_ref[r, :] * (force_ref[step, r, :] - level)
            lev_copy(step, piece).start()
        @pl.when(opening)
        def _():
            inputs[11].wait()
            hi, lo = halves(gradw_ref[...])
            for half_w, local_w in ((hi, gl_hi), (lo, gl_lo)):
                slot = [half_w[sl(k, cells), :] for k in range(5)]
                for h in (0, 1):
                    local_w[h] = jnp.concatenate(slot[:3] + [slot[4 - h]], axis=0)
            for h in (0, 1):
                gs_twice[h] = jnp.concatenate([hi[sl(3 + h, cells), :]] * 2, axis=0)
                gs_lo[h] = lo[sl(3 + h, cells), :]
        hi, lo = halves(lev_send[step + 1])

        @pl.when(closing)
        def _():
            migrate(0, hi, lo)

        near = mm(near_rows[...], jnp.concatenate([hi, lo], axis=1)).astype(bf16)
        near = [near[sl(k, blocks)] for k in range(3)]
        hi4 = jnp.concatenate([hi] + [p[:, :cells] for p in near], axis=1)
        lo4 = jnp.concatenate([lo] + [p[:, cells:] for p in near], axis=1)
        for h in (0, 1):
            r = sl(h, half)
            grad_ref[r, :] = mm3(hi4[r], lo4[r], gl_hi[h], gl_lo[h])

        @pl.when(opening)
        def _():
            choose()

        for piece in near_pieces + far_pieces:
            h, _, first, size = piece
            r = rows_of(piece)
            lev_copy(step, facing(piece)).wait_recv()
            hi, lo = halves(lev_recv[step, h, first : first + size])
            grad = mm(jnp.concatenate([hi, lo], axis=1), gs_twice[h]) + mm(hi, gs_lo[h])
            grad = grad_ref[r, :] + grad
            depth = depth_p[r, :]
            damp = damp_ref[step, r, cells:]
            x_ref[r, :cells] = damp * (x_ref[r, :cells] - depth * grad[:, :cells])
            x_ref[r, cells:] = damp * (x_ref[r, cells:] - depth * grad[:, cells:])

            @pl.when(jnp.logical_not(closing))
            def _():
                shed(step + 1, piece)
                div_copy(step + 1, piece).start()


    for piece in far_pieces + near_pieces:
        shed(0, piece)

    def step_of(step, _):
        one_step(step)
        return 0

    lax.fori_loop(0, steps, step_of, 0)
    migrate(1, *halves(x_ref[...]))

    def halo_sent(step, _):
        for piece in near_pieces + far_pieces:
            div_copy(step, piece).wait_send()
            lev_copy(step, piece).wait_send()
        return 0

    lax.fori_loop(0, steps, halo_sent, 0)
    all_done(gathered, meta_ss)
    for kind, src, dst in ((0, packed_level, landed_level), (1, packed_flow, landed_flow)):
        own_copy(kind).wait()
        all_done(src, mig_ss.at[kind])
        all_done(dst, mig_rs.at[kind])


def settle(
    slots, moved_hbm, level_hbm, flow_hbm, level_out, flow_out,
    moved_ref, landed_level, landed_flow, level_ref, flow_ref, sem,
):
    copies = [
        pltpu.make_async_copy(src, dst, sem.at[i])
        for i, (src, dst) in enumerate(
            (
                (moved_hbm, moved_ref),
                (level_hbm, landed_level),
                (flow_hbm, landed_flow),
                (level_ref, level_out),
                (flow_ref, flow_out),
            )
        )
    ]
    for copy in copies[:3]:
        copy.start()
    blocks, cells = level_ref.shape
    places = landed_level.shape[0]
    square = (blocks, blocks)
    sub, lane = iota(square, 0), iota(square, 1)
    copies[0].wait()
    owner_row = jnp.floor((moved_ref[...].astype(f32) + 0.5) * (1.0 / blocks))
    owner_col = jnp.sum(jnp.where(sub == lane, owner_row, 0.0), axis=1, keepdims=True)
    ahead = jnp.sum(
        jnp.where(lane < sub, hot(owner_row == owner_col), 0.0), axis=1, keepdims=True
    )
    where_from = owner_col * float(slots) + ahead
    unpack = hot(iota((blocks, places), 1) == where_from).astype(bf16)
    copies[1].wait()
    hi, lo = halves(landed_level[...])
    both = mm(unpack, jnp.concatenate([hi, lo], axis=1))
    level_ref[...] = both[:, :cells] + both[:, cells:]
    copies[3].start()
    copies[2].wait()
    hi, lo = halves(landed_flow[...])
    flow = mm(unpack, hi) + mm(unpack, lo)
    flow_ref[pl.ds(0, blocks, 2), :] = flow[:, :cells]
    flow_ref[pl.ds(1, blocks, 2), :] = flow[:, cells:]
    copies[4].start()
    copies[3].wait()
    copies[4].wait()


def local(
    n,
    elevation,
    momentum,
    depth,
    drag,
    div_weight,
    grad_weight,
    neighbours,
    wet,
    boundary_cells,
    boundary_source,
    series,
    moved_from,
):
    blocks, cells = elevation.shape
    steps, width = series.shape
    half = blocks // 2
    wide = 2 * cells
    portion = 2 * blocks // n
    slots = -(-portion // 8) * 8
    tall = -(-(steps + blocks // width) // 8) * 8
    vmem, dma = pltpu.VMEM, pltpu.SemaphoreType.DMA
    landed_level, landed_flow = pl.pallas_call(
        functools.partial(kernel, n, slots),
        out_shape=(
            jax.ShapeDtypeStruct((n, slots, cells), f32),
            jax.ShapeDtypeStruct((n, slots, wide), f32),
        ),
        in_specs=[pl.BlockSpec(memory_space=pl.ANY)] * 12,
        out_specs=(pl.BlockSpec(memory_space=pl.ANY),) * 2,
        scratch_shapes=[
            vmem((blocks, cells), f32),
            vmem((2 * blocks, cells), f32),
            vmem((blocks, cells), f32),
            vmem((blocks, cells), f32),
            vmem((5 * wide, cells), f32),
            vmem((5 * cells, wide), f32),
            vmem((4, blocks), jnp.int32),
            vmem(wet.shape, jnp.int32),
            vmem((1, boundary_cells.shape[0]), jnp.int32),
            vmem((1, boundary_source.shape[0]), jnp.int32),
            vmem(series.shape, f32),
            vmem((1, blocks), jnp.int32),
            vmem((tall, width), f32),
            vmem((n, tall, width), f32),
            vmem((blocks, wide), f32),
            vmem((3, wide, wide), bf16),
            vmem((3, wide, wide), bf16),
            vmem((2, wide, wide), bf16),
            vmem((2, 4 * cells, wide), bf16),
            vmem((2, 4 * cells, wide), bf16),
            vmem((2, wide, wide), bf16),
            vmem((2, cells, wide), bf16),
            vmem((steps, blocks, wide), f32),
            vmem((blocks, cells), f32),
            vmem((3 * blocks, blocks), bf16),
            vmem((blocks, 3 * blocks), bf16),
            vmem((blocks, cells), f32),
            vmem((blocks, wide), f32),
            vmem((steps, blocks, cells), f32),
            vmem((blocks, cells), f32),
            vmem((steps, 2, half, cells), f32),
            vmem((steps, 2, half, cells), f32),
            vmem((steps + 1, blocks, cells), f32),
            vmem((steps, 2, half, cells), f32),
            vmem((n * slots, blocks), bf16),
            vmem((n, slots, cells), f32),
            vmem((n, slots, wide), f32),
            dma((12,)),
            dma,
            dma,
            dma((steps, 2, 2)),
            dma((steps, 2, 2)),
            dma((steps, 2, 2)),
            dma((steps, 2, 2)),
            dma((2,)),
            dma((2,)),
            dma((2,)),
        ],
        compiler_params=pltpu.CompilerParams(
            collective_id=0, has_side_effects=True, vmem_limit_bytes=60 * 1024 * 1024
        ),
        name="surge",
    )(
        elevation,
        momentum.reshape(2 * blocks, cells),
        depth,
        drag,
        div_weight.reshape(5 * wide, cells),
        grad_weight.reshape(5 * cells, wide),
        neighbours.T,
        wet,
        boundary_cells.reshape(1, -1),
        boundary_source.reshape(1, -1),
        series,
        moved_from.reshape(1, -1),
    )
    level, flow = pl.pallas_call(
        functools.partial(settle, slots),
        out_shape=(
            jax.ShapeDtypeStruct((blocks, cells), f32),
            jax.ShapeDtypeStruct((2 * blocks, cells), f32),
        ),
        in_specs=[pl.BlockSpec(memory_space=pl.ANY)] * 3,
        out_specs=(pl.BlockSpec(memory_space=pl.ANY),) * 2,
        scratch_shapes=[
            vmem((1, blocks), jnp.int32),
            vmem((n * slots, cells), f32),
            vmem((n * slots, wide), f32),
            vmem((blocks, cells), f32),
            vmem((2 * blocks, cells), f32),
            dma((5,)),
        ],
        compiler_params=pltpu.CompilerParams(vmem_limit_bytes=60 * 1024 * 1024),
        name="settle",
    )(
        moved_from.reshape(1, -1),
        landed_level.reshape(n * slots, cells),
        landed_flow.reshape(n * slots, wide),
    )
    return level, flow.reshape(blocks, 2, cells)


def solution(mesh):
    n = mesh.shape["dom"]
    return jax.shard_map(
        functools.partial(local, n),
        mesh=mesh,
        in_specs=(
            P("dom", None),
            P("dom", None, None),
            P("dom", None),
            P("dom", None),
            P(),
            P(),
            P("dom", None),
            P(None, "dom"),
            P("dom"),
            P("dom"),
            P(None, "dom"),
            P("dom"),
        ),
        out_specs=(P("dom", None), P("dom", None, None)),
        check_vma=False,
    )
```

```python
import functools

import jax
import jax.numpy as jnp
from jax import lax
from jax.experimental import pallas as pl
from jax.experimental.pallas import tpu as pltpu
from jax.sharding import PartitionSpec as P

MESH = pl.DeviceIdType.MESH
f32 = jnp.float32
bf16 = jnp.bfloat16
relax_rate = 0.5


def halves(x):
    hi = x.astype(bf16)
    return hi, (x - hi.astype(f32)).astype(bf16)


def mm(a, b):
    return jnp.dot(a, b, preferred_element_type=f32)


def mm3(hi, lo, w_hi, w_lo):
    return mm(hi, w_hi) + (mm(lo, w_hi) + mm(hi, w_lo))


def hot(cond):
    return jnp.where(cond, 1.0, 0.0).astype(f32)


def iota(shape, dim):
    return lax.broadcasted_iota(jnp.int32, shape, dim).astype(f32)


def kernel(
    n, slots,
    elev_hbm, mom_hbm, depth_hbm, drag_hbm, divw_hbm, gradw_hbm, nb_hbm, wet_hbm,
    cells_hbm, source_hbm, series_hbm, moved_hbm,
    landed_level, landed_flow,
    elev_ref, mom_ref, depth_ref, drag_ref, divw_ref, gradw_ref, nb_ref, wet_ref,
    cells_ref, source_ref, series_ref, moved_ref,
    meta, gathered, x_ref, dl_hi, dl_lo, ds_both, gl_hi, gl_lo, gs_twice, gs_lo,
    damp_ref, depth_p, near_rows, near_cols, div_ref, grad_ref,
    found_ref, rows_ref, columns_ref, force_ref, relax_ref, div_send, div_recv, lev_send, lev_recv, pack, packed_level, packed_flow,
    in_ss, meta_ss, meta_rs, div_ss, div_rs, lev_ss, lev_rs, mig_ss, mig_rs, own_ss,
):
    me = lax.axis_index("dom")
    steps, width = series_ref.shape
    blocks, cells = elev_ref.shape
    half = blocks // 2
    wide = 2 * cells
    span = blocks // width

    inputs = [
        pltpu.make_async_copy(src, dst, in_ss.at[i])
        for i, (src, dst) in enumerate(
            (
                (nb_hbm, nb_ref),
                (moved_hbm, moved_ref),
                (series_hbm, series_ref),
                (wet_hbm, wet_ref),
                (cells_hbm, cells_ref),
                (source_hbm, source_ref),
                (mom_hbm, mom_ref),
                (elev_hbm, elev_ref),
                (depth_hbm, depth_ref),
                (drag_hbm, drag_ref),
                (divw_hbm, divw_ref),
                (gradw_hbm, gradw_ref),
            )
        )
    ]
    for copy in inputs:
        copy.start()

    barrier = pltpu.get_barrier_semaphore()

    def greet(i, _):
        pl.semaphore_signal(
            barrier, inc=1, device_id=(lax.rem(me + i, n),), device_id_type=MESH
        )
        return 0

    lax.fori_loop(1, n, greet, 0)

    bits = n.bit_length() - 1
    flips = [(1 - 2 * lax.rem(lax.div(me, 1 << k), 2)) * (1 << k) for k in range(bits)]

    def partner(i):
        j = i - 1
        m = lax.div(j + 1, 2) + (1 - lax.rem(j, 2)) * (n // 2)
        if n != 1 << bits:
            return lax.rem(me + m, n)
        return me + sum(lax.rem(lax.div(m, 1 << k), 2) * flips[k] for k in range(bits))

    def sl(k, size):
        return slice(k * size, (k + 1) * size)

    near_half, far_half = 1 - lax.rem(me, 2), lax.rem(me, 2)

    near_pieces = [(near_half, 0, 0, half)]
    far_pieces = [(far_half, i, i * (half // 2), half // 2) for i in (0, 1)]

    def rows_of(piece):
        h, _, first, size = piece
        return pl.ds(pl.multiple_of(h * half + first, half // 2), size)

    for copy in inputs[:6]:
        copy.wait()
    base = (me * blocks).astype(f32)
    square = (blocks, blocks)
    sub, lane = iota(square, 0), iota(square, 1)
    nb = nb_ref[...].astype(f32)
    nbl = nb - base
    lower_own = jnp.logical_and(nbl[2:3] >= 0.0, nbl[2:3] < float(blocks))
    key_row = jnp.where(lower_own, nb[3:4] + float(blocks), lane[0:1])
    key_col = jnp.sum(jnp.where(sub == lane, key_row, 0.0), axis=1, keepdims=True)
    pos_row = jnp.sum(hot(key_col < key_row), axis=0, keepdims=True)
    pos_col = jnp.sum(hot(key_row < key_col), axis=1, keepdims=True)
    order = hot(sub == pos_row)
    order16 = order.astype(bf16)

    inputs[6].wait()
    hi, lo = halves(
        jnp.concatenate(
            [mom_ref[pl.ds(0, blocks, 2), :], mom_ref[pl.ds(1, blocks, 2), :]], axis=1
        )
    )
    x_ref[...] = mm(order16, hi) + mm(order16, lo)
    inputs[10].wait()
    for h in (0, 1):
        hi, lo = halves(divw_ref[sl(4 - h, wide), :])
        ds_both[h] = jnp.concatenate([hi, lo], axis=1)

    def halo(src, recv, ss, rs, step, piece):
        h, i, first, size = piece
        return pltpu.make_async_remote_copy(
            src_ref=src,
            dst_ref=recv.at[step, 1 - h, pl.ds(first, size)],
            send_sem=ss.at[step, h, i],
            recv_sem=rs.at[step, 1 - h, i],
            device_id=(lax.rem(me + 2 * h - 1 + n, n),),
            device_id_type=MESH,
        )

    def div_copy(step, piece):
        h, _, first, size = piece
        src = div_send.at[step, h, pl.ds(first, size)]
        return halo(src, div_recv, div_ss, div_rs, step, piece)

    def lev_copy(step, piece):
        src = lev_send.at[step + 1, rows_of(piece)]
        return halo(src, lev_recv, lev_ss, lev_rs, step, piece)

    def facing(piece):
        return (1 - piece[0],) + piece[1:]

    def shed(step, piece):
        h, _, first, size = piece
        hi, lo = halves(x_ref[rows_of(piece), :])
        both = mm(hi, ds_both[h])
        rest = mm(lo, ds_both[h, :, :cells])
        div_send[step, h, first : first + size] = both[:, :cells] + (both[:, cells:] + rest)

    def tile_copy(target, source):
        return pltpu.make_async_remote_copy(
            src_ref=meta,
            dst_ref=gathered.at[source],
            send_sem=meta_ss,
            recv_sem=meta_rs,
            device_id=(target,),
            device_id_type=MESH,
        )

    def state_copy(kind, target, source):
        src, dst = ((packed_level, landed_level), (packed_flow, landed_flow))[kind]
        return pltpu.make_async_remote_copy(
            src_ref=src.at[target],
            dst_ref=dst.at[source],
            send_sem=mig_ss.at[kind],
            recv_sem=mig_rs.at[kind],
            device_id=(target,),
            device_id_type=MESH,
        )

    def all_done(ref, sem):
        others = ref.at[pl.ds(0, n - 1)]
        pltpu.make_async_copy(others, others, sem).wait()

    def own_copy(kind):
        src, dst = ((packed_level, landed_level), (packed_flow, landed_flow))[kind]
        return pltpu.make_async_copy(src.at[me], dst.at[me], own_ss.at[kind])

    def migrate(kind, hi, lo):
        src = (packed_level, packed_flow)[kind]
        src[...] = (mm(pack[...], hi) + mm(pack[...], lo)).reshape(src.shape)

        def send(i, _):
            state_copy(kind, partner(i), me).start()
            return 0

        lax.fori_loop(1, n, send, 0)
        own_copy(kind).start()

    moved = moved_ref[...].astype(f32)

    def open_up():
        meta[...] = jnp.zeros_like(meta)
        meta[0:steps, :] = series_ref[...]
        for i in range(span):
            meta[steps + i : steps + i + 1, :] = moved[:, i * width : (i + 1) * width]
        gathered[pl.ds(me, 1)] = meta[...][None]
        pl.semaphore_wait(barrier, n - 1)

    def send_tiles():
        def send(i, _):
            tile_copy(partner(i), me).start()
            return 0

        lax.fori_loop(1, n, send, 0)

        def place(ids):
            return jnp.sum(jnp.where(sub == ids, pos_col, 0.0), axis=0, keepdims=True)

        vertical = jnp.where(lower_own, nbl[2:3], nbl[3:4])
        for k, ids in enumerate((nbl[0:1], nbl[1:2], vertical)):
            col = jnp.sum(order * place(ids), axis=1, keepdims=True)
            near = hot(lane == col).astype(bf16)
            near_rows[sl(k, blocks), :] = near
            near_cols[:, sl(k, blocks)] = near
        for copy in inputs[7:10]:
            copy.wait()
        hi, lo = halves(jnp.concatenate([elev_ref[...], depth_ref[...], drag_ref[...]], axis=1))
        field = mm(order16, hi) + mm(order16, lo)
        lev_send[0] = field[:, :cells]
        depth_p[...] = field[:, cells : 2 * cells]
        damping = 1.0 / (1.0 + field[:, 2 * cells :])
        hi, lo = halves(divw_ref[...])
        for half_w, local_w in ((hi, dl_hi), (lo, dl_lo)):
            slot = [half_w[sl(k, wide), :] for k in range(5)]
            local_w[0] = jnp.concatenate([slot[0], slot[1]], axis=1)
            for h in (0, 1):
                local_w[1 + h] = jnp.concatenate([slot[2], slot[3 + h]], axis=1)
        wet = wet_ref[...].astype(f32)
        for s in range(steps):
            mask = jnp.sum(order * wet[s : s + 1], axis=1, keepdims=True)
            damp_ref[s, :, :cells] = jnp.broadcast_to(mask, (blocks, cells))
            damp_ref[s, :, cells:] = mask * damping

    def spread(values):
        return lax.dot_general(
            rows_ref[...], values, (((1,), (1,)), ((), ())), preferred_element_type=f32
        )

    def force(step):
        hi, lo = halves(columns_ref[...] * found_ref[pl.ds(step, 1), :])
        force_ref[step] = spread(hi) + spread(lo)

    def boundary():
        entries = cells_ref.shape[1]
        point = source_ref[...].astype(f32)
        chunk = jnp.floor((point + 0.5) * (1.0 / width))
        spot = point - chunk * width
        pick = hot(iota((width, entries), 0) == spot).astype(bf16)
        cell = cells_ref[...].astype(f32)
        block = jnp.floor((cell + 0.5) * (1.0 / cells))
        element = cell - block * cells
        block_place = jnp.sum(
            jnp.where(iota((blocks, entries), 0) == block, pos_col, 0.0), axis=0, keepdims=True
        )
        rows = hot(iota((blocks, entries), 0) == block_place).astype(bf16)
        columns = hot(iota((cells, entries), 0) == element)

        rows_ref[...] = rows
        columns_ref[...] = columns
        relax_ref[...] = relax_rate * spread(columns.astype(bf16))

        all_done(gathered, meta_rs)
        tall = meta.shape[0]
        hi, lo = halves(gathered[...].reshape(n * tall, width))
        found = (mm(hi, pick) + mm(lo, pick)).reshape(n, tall, entries)
        found_ref[...] = jnp.sum(
            jnp.where(iota(found.shape, 0) == chunk[None], found, 0.0), axis=0
        )

    def choose():
        everyone = gathered[...]
        takes = jnp.concatenate([everyone[:, steps + i, :] for i in range(span)], axis=1) - base
        mine = hot(jnp.logical_and(takes >= 0.0, takes < float(blocks)))
        rank = mm(mine.astype(bf16), hot(sub < lane).astype(bf16))
        rank = jnp.where(mine > 0.0, rank, -1.0)
        cube = (n, slots, blocks)
        chosen = jnp.where(rank[:, None, :] == iota(cube, 1), takes[:, None, :] + 1.0, 0.0)
        chosen = jnp.sum(chosen.reshape(n * slots, blocks), axis=1, keepdims=True) - 1.0
        lanes = iota((n * slots, blocks), 1)
        pack[...] = mm(
            hot(lanes == chosen).astype(bf16), hot(lane == pos_col).astype(bf16)
        ).astype(bf16)

    def one_step(step):
        opening, closing = step == 0, step == steps - 1

        @pl.when(opening)
        def _():
            open_up()
            for piece in far_pieces + near_pieces:
                div_copy(step, piece).start()
            send_tiles()
        hi, lo = halves(x_ref[...])
        first = mm3(hi, lo, dl_hi[0], dl_lo[0])
        second = jnp.concatenate(
            [
                mm3(hi[sl(h, half)], lo[sl(h, half)], dl_hi[1 + h], dl_lo[1 + h])
                for h in (0, 1)
            ],
            axis=0,
        )
        parts = jnp.concatenate([first[:, cells:], second[:, :cells], second[:, cells:]], axis=0)
        parts = mm(near_cols[...], jnp.concatenate(halves(parts), axis=1))
        div_ref[...] = first[:, :cells] + (parts[:, :cells] + parts[:, cells:])
        @pl.when(opening)
        def _():
            boundary()
            force(0)

        @pl.when(step == min(1, steps - 1))
        def _():
            choose()

        for piece in near_pieces + far_pieces:
            h, _, first, size = piece
            r = rows_of(piece)
            div_copy(step, facing(piece)).wait_recv()
            div = div_ref[r, :] + div_recv[step, h, first : first + size]
            level = lev_send[step, r, :] - damp_ref[step, r, :cells] * div
            lev_send[step + 1, r, :] = level + relax_ref[r, :] * (force_ref[step, r, :] - level)
            lev_copy(step, piece).start()
        @pl.when(opening)
        def _():
            inputs[11].wait()
            hi, lo = halves(gradw_ref[...])
            for half_w, local_w in ((hi, gl_hi), (lo, gl_lo)):
                slot = [half_w[sl(k, cells), :] for k in range(5)]
                for h in (0, 1):
                    local_w[h] = jnp.concatenate(slot[:3] + [slot[4 - h]], axis=0)
            for h in (0, 1):
                gs_twice[h] = jnp.concatenate([hi[sl(3 + h, cells), :]] * 2, axis=0)
                gs_lo[h] = lo[sl(3 + h, cells), :]
        hi, lo = halves(lev_send[step + 1])

        @pl.when(closing)
        def _():
            migrate(0, hi, lo)

        near = mm(near_rows[...], jnp.concatenate([hi, lo], axis=1)).astype(bf16)
        near = [near[sl(k, blocks)] for k in range(3)]
        hi4 = jnp.concatenate([hi] + [p[:, :cells] for p in near], axis=1)
        lo4 = jnp.concatenate([lo] + [p[:, cells:] for p in near], axis=1)
        for h in (0, 1):
            r = sl(h, half)
            grad_ref[r, :] = mm3(hi4[r], lo4[r], gl_hi[h], gl_lo[h])

        @pl.when(jnp.logical_not(closing))
        def _():
            force(step + 1)

        for piece in near_pieces + far_pieces:
            h, _, first, size = piece
            r = rows_of(piece)
            lev_copy(step, facing(piece)).wait_recv()
            hi, lo = halves(lev_recv[step, h, first : first + size])
            grad = mm(jnp.concatenate([hi, lo], axis=1), gs_twice[h]) + mm(hi, gs_lo[h])
            grad = grad_ref[r, :] + grad
            depth = depth_p[r, :]
            damp = damp_ref[step, r, cells:]
            x_ref[r, :cells] = damp * (x_ref[r, :cells] - depth * grad[:, :cells])
            x_ref[r, cells:] = damp * (x_ref[r, cells:] - depth * grad[:, cells:])

            @pl.when(jnp.logical_not(closing))
            def _():
                shed(step + 1, piece)
                div_copy(step + 1, piece).start()


    for piece in far_pieces + near_pieces:
        shed(0, piece)

    def step_of(step, _):
        one_step(step)
        return 0

    lax.fori_loop(0, steps, step_of, 0)
    migrate(1, *halves(x_ref[...]))

    def halo_sent(step, _):
        for piece in near_pieces + far_pieces:
            div_copy(step, piece).wait_send()
            lev_copy(step, piece).wait_send()
        return 0

    lax.fori_loop(0, steps, halo_sent, 0)
    all_done(gathered, meta_ss)
    for kind, src, dst in ((0, packed_level, landed_level), (1, packed_flow, landed_flow)):
        own_copy(kind).wait()
        all_done(src, mig_ss.at[kind])
        all_done(dst, mig_rs.at[kind])


def settle(
    slots, moved_hbm, level_hbm, flow_hbm, level_out, flow_out,
    moved_ref, landed_level, landed_flow, level_ref, flow_ref, sem,
):
    copies = [
        pltpu.make_async_copy(src, dst, sem.at[i])
        for i, (src, dst) in enumerate(
            (
                (moved_hbm, moved_ref),
                (level_hbm, landed_level),
                (flow_hbm, landed_flow),
                (level_ref, level_out),
                (flow_ref, flow_out),
            )
        )
    ]
    for copy in copies[:3]:
        copy.start()
    blocks, cells = level_ref.shape
    places = landed_level.shape[0]
    square = (blocks, blocks)
    sub, lane = iota(square, 0), iota(square, 1)
    copies[0].wait()
    owner_row = jnp.floor((moved_ref[...].astype(f32) + 0.5) * (1.0 / blocks))
    owner_col = jnp.sum(jnp.where(sub == lane, owner_row, 0.0), axis=1, keepdims=True)
    ahead = jnp.sum(
        jnp.where(lane < sub, hot(owner_row == owner_col), 0.0), axis=1, keepdims=True
    )
    where_from = owner_col * float(slots) + ahead
    unpack = hot(iota((blocks, places), 1) == where_from).astype(bf16)
    copies[1].wait()
    hi, lo = halves(landed_level[...])
    both = mm(unpack, jnp.concatenate([hi, lo], axis=1))
    level_ref[...] = both[:, :cells] + both[:, cells:]
    copies[3].start()
    copies[2].wait()
    hi, lo = halves(landed_flow[...])
    flow = mm(unpack, hi) + mm(unpack, lo)
    flow_ref[pl.ds(0, blocks, 2), :] = flow[:, :cells]
    flow_ref[pl.ds(1, blocks, 2), :] = flow[:, cells:]
    copies[4].start()
    copies[3].wait()
    copies[4].wait()


def local(
    n,
    elevation,
    momentum,
    depth,
    drag,
    div_weight,
    grad_weight,
    neighbours,
    wet,
    boundary_cells,
    boundary_source,
    series,
    moved_from,
):
    blocks, cells = elevation.shape
    steps, width = series.shape
    half = blocks // 2
    wide = 2 * cells
    portion = 2 * blocks // n
    slots = -(-portion // 8) * 8
    tall = -(-(steps + blocks // width) // 8) * 8
    vmem, dma = pltpu.VMEM, pltpu.SemaphoreType.DMA
    landed_level, landed_flow = pl.pallas_call(
        functools.partial(kernel, n, slots),
        out_shape=(
            jax.ShapeDtypeStruct((n, slots, cells), f32),
            jax.ShapeDtypeStruct((n, slots, wide), f32),
        ),
        in_specs=[pl.BlockSpec(memory_space=pl.ANY)] * 12,
        out_specs=(pl.BlockSpec(memory_space=pl.ANY),) * 2,
        scratch_shapes=[
            vmem((blocks, cells), f32),
            vmem((2 * blocks, cells), f32),
            vmem((blocks, cells), f32),
            vmem((blocks, cells), f32),
            vmem((5 * wide, cells), f32),
            vmem((5 * cells, wide), f32),
            vmem((4, blocks), jnp.int32),
            vmem(wet.shape, jnp.int32),
            vmem((1, boundary_cells.shape[0]), jnp.int32),
            vmem((1, boundary_source.shape[0]), jnp.int32),
            vmem(series.shape, f32),
            vmem((1, blocks), jnp.int32),
            vmem((tall, width), f32),
            vmem((n, tall, width), f32),
            vmem((blocks, wide), f32),
            vmem((3, wide, wide), bf16),
            vmem((3, wide, wide), bf16),
            vmem((2, wide, wide), bf16),
            vmem((2, 4 * cells, wide), bf16),
            vmem((2, 4 * cells, wide), bf16),
            vmem((2, wide, wide), bf16),
            vmem((2, cells, wide), bf16),
            vmem((steps, blocks, wide), f32),
            vmem((blocks, cells), f32),
            vmem((3 * blocks, blocks), bf16),
            vmem((blocks, 3 * blocks), bf16),
            vmem((blocks, cells), f32),
            vmem((blocks, wide), f32),
            vmem((tall, boundary_cells.shape[0]), f32),
            vmem((blocks, boundary_cells.shape[0]), bf16),
            vmem((cells, boundary_cells.shape[0]), f32),
            vmem((steps, blocks, cells), f32),
            vmem((blocks, cells), f32),
            vmem((steps, 2, half, cells), f32),
            vmem((steps, 2, half, cells), f32),
            vmem((steps + 1, blocks, cells), f32),
            vmem((steps, 2, half, cells), f32),
            vmem((n * slots, blocks), bf16),
            vmem((n, slots, cells), f32),
            vmem((n, slots, wide), f32),
            dma((12,)),
            dma,
            dma,
            dma((steps, 2, 2)),
            dma((steps, 2, 2)),
            dma((steps, 2, 2)),
            dma((steps, 2, 2)),
            dma((2,)),
            dma((2,)),
            dma((2,)),
        ],
        compiler_params=pltpu.CompilerParams(
            collective_id=0, has_side_effects=True, vmem_limit_bytes=60 * 1024 * 1024
        ),
        name="surge",
    )(
        elevation,
        momentum.reshape(2 * blocks, cells),
        depth,
        drag,
        div_weight.reshape(5 * wide, cells),
        grad_weight.reshape(5 * cells, wide),
        neighbours.T,
        wet,
        boundary_cells.reshape(1, -1),
        boundary_source.reshape(1, -1),
        series,
        moved_from.reshape(1, -1),
    )
    level, flow = pl.pallas_call(
        functools.partial(settle, slots),
        out_shape=(
            jax.ShapeDtypeStruct((blocks, cells), f32),
            jax.ShapeDtypeStruct((2 * blocks, cells), f32),
        ),
        in_specs=[pl.BlockSpec(memory_space=pl.ANY)] * 3,
        out_specs=(pl.BlockSpec(memory_space=pl.ANY),) * 2,
        scratch_shapes=[
            vmem((1, blocks), jnp.int32),
            vmem((n * slots, cells), f32),
            vmem((n * slots, wide), f32),
            vmem((blocks, cells), f32),
            vmem((2 * blocks, cells), f32),
            dma((5,)),
        ],
        compiler_params=pltpu.CompilerParams(vmem_limit_bytes=60 * 1024 * 1024),
        name="settle",
    )(
        moved_from.reshape(1, -1),
        landed_level.reshape(n * slots, cells),
        landed_flow.reshape(n * slots, wide),
    )
    return level, flow.reshape(blocks, 2, cells)


def solution(mesh):
    n = mesh.shape["dom"]
    return jax.shard_map(
        functools.partial(local, n),
        mesh=mesh,
        in_specs=(
            P("dom", None),
            P("dom", None, None),
            P("dom", None),
            P("dom", None),
            P(),
            P(),
            P("dom", None),
            P(None, "dom"),
            P("dom"),
            P("dom"),
            P(None, "dom"),
            P("dom"),
        ),
        out_specs=(P("dom", None), P("dom", None, None)),
        check_vma=False,
    )
```

```python
import functools

import jax
import jax.numpy as jnp
from jax import lax
from jax.experimental import pallas as pl
from jax.experimental.pallas import tpu as pltpu
from jax.sharding import PartitionSpec as P

MESH = pl.DeviceIdType.MESH
f32 = jnp.float32
bf16 = jnp.bfloat16
relax_rate = 0.5


def halves(x):
    hi = x.astype(bf16)
    return hi, (x - hi.astype(f32)).astype(bf16)


def mm(a, b):
    return jnp.dot(a, b, preferred_element_type=f32)


def mm3(hi, lo, w_hi, w_lo):
    return mm(hi, w_hi) + (mm(lo, w_hi) + mm(hi, w_lo))


def hot(cond):
    return jnp.where(cond, 1.0, 0.0).astype(f32)


def iota(shape, dim):
    return lax.broadcasted_iota(jnp.int32, shape, dim).astype(f32)


def kernel(
    n, slots,
    elev_hbm, mom_hbm, depth_hbm, drag_hbm, divw_hbm, gradw_hbm, nb_hbm, wet_hbm,
    cells_hbm, source_hbm, series_hbm, moved_hbm,
    landed_level, landed_flow,
    elev_ref, mom_ref, depth_ref, drag_ref, divw_ref, gradw_ref, nb_ref, wet_ref,
    cells_ref, source_ref, series_ref, moved_ref,
    meta, gathered, x_ref, dl_hi, dl_lo, ds_both, gl_hi, gl_lo, gs_twice, gs_lo,
    damp_ref, depth_p, near_rows, near_cols, div_ref, grad_ref,
    force_ref, relax_ref, div_send, div_recv, lev_send, lev_recv, pack, packed_level, packed_flow,
    in_ss, meta_ss, meta_rs, div_ss, div_rs, lev_ss, lev_rs, mig_ss, mig_rs, own_ss,
):
    me = lax.axis_index("dom")
    steps, width = series_ref.shape
    blocks, cells = elev_ref.shape
    half = blocks // 2
    wide = 2 * cells
    span = blocks // width

    inputs = [
        pltpu.make_async_copy(src, dst, in_ss.at[i])
        for i, (src, dst) in enumerate(
            (
                (nb_hbm, nb_ref),
                (moved_hbm, moved_ref),
                (series_hbm, series_ref),
                (wet_hbm, wet_ref),
                (cells_hbm, cells_ref),
                (source_hbm, source_ref),
                (mom_hbm, mom_ref),
                (elev_hbm, elev_ref),
                (depth_hbm, depth_ref),
                (drag_hbm, drag_ref),
                (divw_hbm, divw_ref),
                (gradw_hbm, gradw_ref),
            )
        )
    ]
    for copy in inputs:
        copy.start()

    barrier = pltpu.get_barrier_semaphore()

    def greet(i, _):
        pl.semaphore_signal(
            barrier, inc=1, device_id=(lax.rem(me + i, n),), device_id_type=MESH
        )
        return 0

    lax.fori_loop(1, n, greet, 0)

    bits = n.bit_length() - 1
    flips = [(1 - 2 * lax.rem(lax.div(me, 1 << k), 2)) * (1 << k) for k in range(bits)]

    def partner(i):
        m = i // 2 + (i % 2) * (n // 2)
        if n != 1 << bits:
            return lax.rem(me + m, n)
        return me + sum(flips[k] for k in range(bits) if m >> k & 1)

    def sl(k, size):
        return slice(k * size, (k + 1) * size)

    near_half, far_half = 1 - lax.rem(me, 2), lax.rem(me, 2)

    near_pieces = [(near_half, 0, 0, half)]
    far_pieces = [(far_half, i, i * (half // 2), half // 2) for i in (0, 1)]

    def rows_of(piece):
        h, _, first, size = piece
        return pl.ds(pl.multiple_of(h * half + first, half // 2), size)

    for copy in inputs[:6]:
        copy.wait()
    base = (me * blocks).astype(f32)
    square = (blocks, blocks)
    sub, lane = iota(square, 0), iota(square, 1)
    nb = nb_ref[...].astype(f32)
    nbl = nb - base
    lower_own = jnp.logical_and(nbl[2:3] >= 0.0, nbl[2:3] < float(blocks))
    key_row = jnp.where(lower_own, nb[3:4] + float(blocks), lane[0:1])
    key_col = jnp.sum(jnp.where(sub == lane, key_row, 0.0), axis=1, keepdims=True)
    pos_row = jnp.sum(hot(key_col < key_row), axis=0, keepdims=True)
    pos_col = jnp.sum(hot(key_row < key_col), axis=1, keepdims=True)
    order = hot(sub == pos_row)
    order16 = order.astype(bf16)

    inputs[6].wait()
    hi, lo = halves(
        jnp.concatenate(
            [mom_ref[pl.ds(0, blocks, 2), :], mom_ref[pl.ds(1, blocks, 2), :]], axis=1
        )
    )
    x_ref[...] = mm(order16, hi) + mm(order16, lo)
    inputs[10].wait()
    for h in (0, 1):
        hi, lo = halves(divw_ref[sl(4 - h, wide), :])
        ds_both[h] = jnp.concatenate([hi, lo], axis=1)

    def halo(src, recv, ss, rs, step, piece):
        h, i, first, size = piece
        return pltpu.make_async_remote_copy(
            src_ref=src,
            dst_ref=recv.at[step, 1 - h, pl.ds(first, size)],
            send_sem=ss.at[step, h, i],
            recv_sem=rs.at[step, 1 - h, i],
            device_id=(lax.rem(me + 2 * h - 1 + n, n),),
            device_id_type=MESH,
        )

    def div_copy(step, piece):
        h, _, first, size = piece
        src = div_send.at[step, h, pl.ds(first, size)]
        return halo(src, div_recv, div_ss, div_rs, step, piece)

    def lev_copy(step, piece):
        src = lev_send.at[step + 1, rows_of(piece)]
        return halo(src, lev_recv, lev_ss, lev_rs, step, piece)

    def facing(piece):
        return (1 - piece[0],) + piece[1:]

    def shed(step, piece):
        h, _, first, size = piece
        hi, lo = halves(x_ref[rows_of(piece), :])
        both = mm(hi, ds_both[h])
        rest = mm(lo, ds_both[h, :, :cells])
        div_send[step, h, first : first + size] = both[:, :cells] + (both[:, cells:] + rest)

    def tile_copy(target, source):
        return pltpu.make_async_remote_copy(
            src_ref=meta,
            dst_ref=gathered.at[source],
            send_sem=meta_ss,
            recv_sem=meta_rs,
            device_id=(target,),
            device_id_type=MESH,
        )

    def state_copy(kind, target, source):
        src, dst = ((packed_level, landed_level), (packed_flow, landed_flow))[kind]
        return pltpu.make_async_remote_copy(
            src_ref=src.at[target],
            dst_ref=dst.at[source],
            send_sem=mig_ss.at[kind],
            recv_sem=mig_rs.at[kind],
            device_id=(target,),
            device_id_type=MESH,
        )

    def all_done(ref, sem):
        others = ref.at[pl.ds(0, n - 1)]
        pltpu.make_async_copy(others, others, sem).wait()

    def own_copy(kind):
        src, dst = ((packed_level, landed_level), (packed_flow, landed_flow))[kind]
        return pltpu.make_async_copy(src.at[me], dst.at[me], own_ss.at[kind])

    def migrate(kind, hi, lo):
        src = (packed_level, packed_flow)[kind]
        src[...] = (mm(pack[...], hi) + mm(pack[...], lo)).reshape(src.shape)

        for i in range(1, n):
            state_copy(kind, partner(i), me).start()
        own_copy(kind).start()

    moved = moved_ref[...].astype(f32)

    def open_up():
        meta[...] = jnp.zeros_like(meta)
        meta[0:steps, :] = series_ref[...]
        for i in range(span):
            meta[steps + i : steps + i + 1, :] = moved[:, i * width : (i + 1) * width]
        gathered[pl.ds(me, 1)] = meta[...][None]
        pl.semaphore_wait(barrier, n - 1)

    def send_tiles():
        for i in range(1, n):
            tile_copy(partner(i), me).start()

        def place(ids):
            return jnp.sum(jnp.where(sub == ids, pos_col, 0.0), axis=0, keepdims=True)

        vertical = jnp.where(lower_own, nbl[2:3], nbl[3:4])
        for k, ids in enumerate((nbl[0:1], nbl[1:2], vertical)):
            col = jnp.sum(order * place(ids), axis=1, keepdims=True)
            near = hot(lane == col).astype(bf16)
            near_rows[sl(k, blocks), :] = near
            near_cols[:, sl(k, blocks)] = near
        for copy in inputs[7:10]:
            copy.wait()
        hi, lo = halves(jnp.concatenate([elev_ref[...], depth_ref[...], drag_ref[...]], axis=1))
        field = mm(order16, hi) + mm(order16, lo)
        lev_send[0] = field[:, :cells]
        depth_p[...] = field[:, cells : 2 * cells]
        damping = 1.0 / (1.0 + field[:, 2 * cells :])
        hi, lo = halves(divw_ref[...])
        for half_w, local_w in ((hi, dl_hi), (lo, dl_lo)):
            slot = [half_w[sl(k, wide), :] for k in range(5)]
            local_w[0] = jnp.concatenate([slot[0], slot[1]], axis=1)
            for h in (0, 1):
                local_w[1 + h] = jnp.concatenate([slot[2], slot[3 + h]], axis=1)
        wet = wet_ref[...].astype(f32)
        for s in range(steps):
            mask = jnp.sum(order * wet[s : s + 1], axis=1, keepdims=True)
            damp_ref[s, :, :cells] = jnp.broadcast_to(mask, (blocks, cells))
            damp_ref[s, :, cells:] = mask * damping

    def boundary():
        entries = cells_ref.shape[1]
        point = source_ref[...].astype(f32)
        chunk = jnp.floor((point + 0.5) * (1.0 / width))
        spot = point - chunk * width
        pick = hot(iota((width, entries), 0) == spot).astype(bf16)
        cell = cells_ref[...].astype(f32)
        block = jnp.floor((cell + 0.5) * (1.0 / cells))
        element = cell - block * cells
        block_place = jnp.sum(
            jnp.where(iota((blocks, entries), 0) == block, pos_col, 0.0), axis=0, keepdims=True
        )
        rows = hot(iota((blocks, entries), 0) == block_place).astype(bf16)
        columns = hot(iota((cells, entries), 0) == element)

        def spread(values):
            return lax.dot_general(
                rows, values, (((1,), (1,)), ((), ())), preferred_element_type=f32
            )

        relax_ref[...] = relax_rate * spread(columns.astype(bf16))

        all_done(gathered, meta_rs)
        tall = meta.shape[0]
        hi, lo = halves(gathered[...].reshape(n * tall, width))
        found = (mm(hi, pick) + mm(lo, pick)).reshape(n, tall, entries)
        found = jnp.sum(jnp.where(iota(found.shape, 0) == chunk[None], found, 0.0), axis=0)

        def force(s):
            hi, lo = halves(columns * found[s : s + 1])
            force_ref[s] = spread(hi) + spread(lo)

        force(0)
        return force

    def choose():
        everyone = gathered[...]
        takes = jnp.concatenate([everyone[:, steps + i, :] for i in range(span)], axis=1) - base
        mine = hot(jnp.logical_and(takes >= 0.0, takes < float(blocks)))
        rank = mm(mine.astype(bf16), hot(sub < lane).astype(bf16))
        rank = jnp.where(mine > 0.0, rank, -1.0)
        cube = (n, slots, blocks)
        chosen = jnp.where(rank[:, None, :] == iota(cube, 1), takes[:, None, :] + 1.0, 0.0)
        chosen = jnp.sum(chosen.reshape(n * slots, blocks), axis=1, keepdims=True) - 1.0
        lanes = iota((n * slots, blocks), 1)
        pack[...] = mm(
            hot(lanes == chosen).astype(bf16), hot(lane == pos_col).astype(bf16)
        ).astype(bf16)

    def one_step(step):
        opening, closing = step == 0, step == steps - 1

        @pl.when(opening)
        def _():
            open_up()
            for piece in far_pieces + near_pieces:
                div_copy(step, piece).start()
            send_tiles()
        hi, lo = halves(x_ref[...])
        first = mm3(hi, lo, dl_hi[0], dl_lo[0])
        second = jnp.concatenate(
            [
                mm3(hi[sl(h, half)], lo[sl(h, half)], dl_hi[1 + h], dl_lo[1 + h])
                for h in (0, 1)
            ],
            axis=0,
        )
        parts = jnp.concatenate([first[:, cells:], second[:, :cells], second[:, cells:]], axis=0)
        parts = mm(near_cols[...], jnp.concatenate(halves(parts), axis=1))
        div_ref[...] = first[:, :cells] + (parts[:, :cells] + parts[:, cells:])
        @pl.when(opening)
        def _():
            force = boundary()
            for later in range(1, steps):
                force(later)

        for piece in near_pieces + far_pieces:
            h, _, first, size = piece
            r = rows_of(piece)
            div_copy(step, facing(piece)).wait_recv()
            div = div_ref[r, :] + div_recv[step, h, first : first + size]
            level = lev_send[step, r, :] - damp_ref[step, r, :cells] * div
            lev_send[step + 1, r, :] = level + relax_ref[r, :] * (force_ref[step, r, :] - level)
            lev_copy(step, piece).start()
        @pl.when(opening)
        def _():
            inputs[11].wait()
            hi, lo = halves(gradw_ref[...])
            for half_w, local_w in ((hi, gl_hi), (lo, gl_lo)):
                slot = [half_w[sl(k, cells), :] for k in range(5)]
                for h in (0, 1):
                    local_w[h] = jnp.concatenate(slot[:3] + [slot[4 - h]], axis=0)
            for h in (0, 1):
                gs_twice[h] = jnp.concatenate([hi[sl(3 + h, cells), :]] * 2, axis=0)
                gs_lo[h] = lo[sl(3 + h, cells), :]
        hi, lo = halves(lev_send[step + 1])

        @pl.when(closing)
        def _():
            migrate(0, hi, lo)

        near = mm(near_rows[...], jnp.concatenate([hi, lo], axis=1)).astype(bf16)
        near = [near[sl(k, blocks)] for k in range(3)]
        hi4 = jnp.concatenate([hi] + [p[:, :cells] for p in near], axis=1)
        lo4 = jnp.concatenate([lo] + [p[:, cells:] for p in near], axis=1)
        for h in (0, 1):
            r = sl(h, half)
            grad_ref[r, :] = mm3(hi4[r], lo4[r], gl_hi[h], gl_lo[h])

        @pl.when(opening)
        def _():
            choose()

        for piece in near_pieces + far_pieces:
            h, _, first, size = piece
            r = rows_of(piece)
            lev_copy(step, facing(piece)).wait_recv()
            hi, lo = halves(lev_recv[step, h, first : first + size])
            grad = mm(jnp.concatenate([hi, lo], axis=1), gs_twice[h]) + mm(hi, gs_lo[h])
            grad = grad_ref[r, :] + grad
            depth = depth_p[r, :]
            damp = damp_ref[step, r, cells:]
            x_ref[r, :cells] = damp * (x_ref[r, :cells] - depth * grad[:, :cells])
            x_ref[r, cells:] = damp * (x_ref[r, cells:] - depth * grad[:, cells:])

            @pl.when(jnp.logical_not(closing))
            def _():
                shed(step + 1, piece)
                div_copy(step + 1, piece).start()


    for piece in far_pieces + near_pieces:
        shed(0, piece)

    def step_of(step, _):
        one_step(step)
        return 0

    lax.fori_loop(0, steps, step_of, 0)
    migrate(1, *halves(x_ref[...]))

    def halo_sent(step, _):
        for piece in near_pieces + far_pieces:
            div_copy(step, piece).wait_send()
            lev_copy(step, piece).wait_send()
        return 0

    lax.fori_loop(0, steps, halo_sent, 0)
    all_done(gathered, meta_ss)
    for kind, src, dst in ((0, packed_level, landed_level), (1, packed_flow, landed_flow)):
        own_copy(kind).wait()
        all_done(src, mig_ss.at[kind])
        all_done(dst, mig_rs.at[kind])


def settle(
    slots, moved_hbm, level_hbm, flow_hbm, level_out, flow_out,
    moved_ref, landed_level, landed_flow, level_ref, flow_ref, sem,
):
    copies = [
        pltpu.make_async_copy(src, dst, sem.at[i])
        for i, (src, dst) in enumerate(
            (
                (moved_hbm, moved_ref),
                (level_hbm, landed_level),
                (flow_hbm, landed_flow),
                (level_ref, level_out),
                (flow_ref, flow_out),
            )
        )
    ]
    for copy in copies[:3]:
        copy.start()
    blocks, cells = level_ref.shape
    places = landed_level.shape[0]
    square = (blocks, blocks)
    sub, lane = iota(square, 0), iota(square, 1)
    copies[0].wait()
    owner_row = jnp.floor((moved_ref[...].astype(f32) + 0.5) * (1.0 / blocks))
    owner_col = jnp.sum(jnp.where(sub == lane, owner_row, 0.0), axis=1, keepdims=True)
    ahead = jnp.sum(
        jnp.where(lane < sub, hot(owner_row == owner_col), 0.0), axis=1, keepdims=True
    )
    where_from = owner_col * float(slots) + ahead
    unpack = hot(iota((blocks, places), 1) == where_from).astype(bf16)
    copies[1].wait()
    hi, lo = halves(landed_level[...])
    both = mm(unpack, jnp.concatenate([hi, lo], axis=1))
    level_ref[...] = both[:, :cells] + both[:, cells:]
    copies[3].start()
    copies[2].wait()
    hi, lo = halves(landed_flow[...])
    flow = mm(unpack, hi) + mm(unpack, lo)
    flow_ref[pl.ds(0, blocks, 2), :] = flow[:, :cells]
    flow_ref[pl.ds(1, blocks, 2), :] = flow[:, cells:]
    copies[4].start()
    copies[3].wait()
    copies[4].wait()


def local(
    n,
    elevation,
    momentum,
    depth,
    drag,
    div_weight,
    grad_weight,
    neighbours,
    wet,
    boundary_cells,
    boundary_source,
    series,
    moved_from,
):
    blocks, cells = elevation.shape
    steps, width = series.shape
    half = blocks // 2
    wide = 2 * cells
    portion = 2 * blocks // n
    slots = -(-portion // 8) * 8
    tall = -(-(steps + blocks // width) // 8) * 8
    vmem, dma = pltpu.VMEM, pltpu.SemaphoreType.DMA
    landed_level, landed_flow = pl.pallas_call(
        functools.partial(kernel, n, slots),
        out_shape=(
            jax.ShapeDtypeStruct((n, slots, cells), f32),
            jax.ShapeDtypeStruct((n, slots, wide), f32),
        ),
        in_specs=[pl.BlockSpec(memory_space=pl.ANY)] * 12,
        out_specs=(pl.BlockSpec(memory_space=pl.ANY),) * 2,
        scratch_shapes=[
            vmem((blocks, cells), f32),
            vmem((2 * blocks, cells), f32),
            vmem((blocks, cells), f32),
            vmem((blocks, cells), f32),
            vmem((5 * wide, cells), f32),
            vmem((5 * cells, wide), f32),
            vmem((4, blocks), jnp.int32),
            vmem(wet.shape, jnp.int32),
            vmem((1, boundary_cells.shape[0]), jnp.int32),
            vmem((1, boundary_source.shape[0]), jnp.int32),
            vmem(series.shape, f32),
            vmem((1, blocks), jnp.int32),
            vmem((tall, width), f32),
            vmem((n, tall, width), f32),
            vmem((blocks, wide), f32),
            vmem((3, wide, wide), bf16),
            vmem((3, wide, wide), bf16),
            vmem((2, wide, wide), bf16),
            vmem((2, 4 * cells, wide), bf16),
            vmem((2, 4 * cells, wide), bf16),
            vmem((2, wide, wide), bf16),
            vmem((2, cells, wide), bf16),
            vmem((steps, blocks, wide), f32),
            vmem((blocks, cells), f32),
            vmem((3 * blocks, blocks), bf16),
            vmem((blocks, 3 * blocks), bf16),
            vmem((blocks, cells), f32),
            vmem((blocks, wide), f32),
            vmem((steps, blocks, cells), f32),
            vmem((blocks, cells), f32),
            vmem((steps, 2, half, cells), f32),
            vmem((steps, 2, half, cells), f32),
            vmem((steps + 1, blocks, cells), f32),
            vmem((steps, 2, half, cells), f32),
            vmem((n * slots, blocks), bf16),
            vmem((n, slots, cells), f32),
            vmem((n, slots, wide), f32),
            dma((12,)),
            dma,
            dma,
            dma((steps, 2, 2)),
            dma((steps, 2, 2)),
            dma((steps, 2, 2)),
            dma((steps, 2, 2)),
            dma((2,)),
            dma((2,)),
            dma((2,)),
        ],
        compiler_params=pltpu.CompilerParams(
            collective_id=0, has_side_effects=True, vmem_limit_bytes=60 * 1024 * 1024
        ),
        name="surge",
    )(
        elevation,
        momentum.reshape(2 * blocks, cells),
        depth,
        drag,
        div_weight.reshape(5 * wide, cells),
        grad_weight.reshape(5 * cells, wide),
        neighbours.T,
        wet,
        boundary_cells.reshape(1, -1),
        boundary_source.reshape(1, -1),
        series,
        moved_from.reshape(1, -1),
    )
    level, flow = pl.pallas_call(
        functools.partial(settle, slots),
        out_shape=(
            jax.ShapeDtypeStruct((blocks, cells), f32),
            jax.ShapeDtypeStruct((2 * blocks, cells), f32),
        ),
        in_specs=[pl.BlockSpec(memory_space=pl.ANY)] * 3,
        out_specs=(pl.BlockSpec(memory_space=pl.ANY),) * 2,
        scratch_shapes=[
            vmem((1, blocks), jnp.int32),
            vmem((n * slots, cells), f32),
            vmem((n * slots, wide), f32),
            vmem((blocks, cells), f32),
            vmem((2 * blocks, cells), f32),
            dma((5,)),
        ],
        compiler_params=pltpu.CompilerParams(vmem_limit_bytes=60 * 1024 * 1024),
        name="settle",
    )(
        moved_from.reshape(1, -1),
        landed_level.reshape(n * slots, cells),
        landed_flow.reshape(n * slots, wide),
    )
    return level, flow.reshape(blocks, 2, cells)


def solution(mesh):
    n = mesh.shape["dom"]
    return jax.shard_map(
        functools.partial(local, n),
        mesh=mesh,
        in_specs=(
            P("dom", None),
            P("dom", None, None),
            P("dom", None),
            P("dom", None),
            P(),
            P(),
            P("dom", None),
            P(None, "dom"),
            P("dom"),
            P("dom"),
            P(None, "dom"),
            P("dom"),
        ),
        out_specs=(P("dom", None), P("dom", None, None)),
        check_vma=False,
    )
```
